768 devices in a mesh: users: 192 (over z, y, core), items: 4 (over x).
Axes of the slice: x: 4, y: 8, z: 12, core: 2. Of those that a mesh axis runs over, the one named last changes fastest.
Arguments:
- block_ids: int32 [768, 4, 8], P('users', 'items'), may hold values from 0 to 191, all different within a row
- pair_live: int32 [768, 4, 8], P('users', 'items'), may hold values from 1 to 64, 320 in all within a row
- user_rows: int32 [768, 4, 8, 64], P('users', 'items'), may hold values from 0 to 127
- item_rows: int32 [768, 4, 8, 64], P('users', 'items'), may hold values from 0 to 127
- counts: int32 [768, 4, 8, 64], P('users', 'items'), may hold values from 1 to 8
- item_emb: float32 [4, 24576, 128], P('items', 'users'), may hold values from -1 to 1
- user_emb: float32 [98304, 128], P('users'), may hold values from -6 to 6
Outputs:
- new_users: float32 [98304, 128], P('users')
The draws below stay inside these ranges and needn't reach their ends.
Inputs may be any that keep to these rules, and one draw needn't show every extreme that they name: `block_ids`: the 8 blocks of one user block and item shard are distinct; every block is named somewhere. `pair_live`: for each user block and item shard the counts sum to 320; the largest is 64.
All inputs are finite; a program needn't handle non-finite values.
Results may differ from the reference program's by a relative error of at most 0.0077.
Values may be sent and summed in bfloat16 or wider, within the bound.
No kernel may reach another device: no remote copies, remote signals or barrier semaphores. Data moves between devices by JAX's collectives and lax.ppermute only.
A program may use at most 32 MiB of HBM per device.

```python
import math
import jax
import jax.numpy as jnp
import numpy as np
from jax import lax

E = 128
BLK = 128
PAIRS = 8
NNZ = 64
ITERS = 3
LIVE = 320
UBLOCKS = 768
USERS = 98304
IROWS = 24576
N_USERS = 192
N_ITEMS = 4


def draw_item_emb(key, part):
    key = jax.random.fold_in(key, 11)
    key_base, key_scale = jax.random.split(key, 2)
    shape = (N_ITEMS, IROWS, E)
    row_scale = jnp.exp(jax.random.uniform(key_scale, (N_ITEMS, IROWS, 1), jnp.float32, math.log(0.2), math.log(2.0)))
    values = jax.random.normal(key_base, shape, jnp.float32)
    values = values * row_scale / math.sqrt(E)
    return jnp.clip(values, -1.0, 1.0).astype(jnp.float32)


def plant(drawn, rng, least, top_value):
    spot = [jax.random.randint(jax.random.fold_in(rng, axis), (), 0, length) for axis, length in enumerate(drawn.shape)]
    main_axis = drawn.shape.index(max(drawn.shape))
    next_to = spot[:main_axis] + [(spot[main_axis] + 1) % drawn.shape[main_axis]] + spot[main_axis + 1:]
    return drawn.at[tuple(spot)].set(least).at[tuple(next_to)].set(top_value)


def block_scale(stream_key, extent, cuts, smallest, top_value):
    gain = 1.0
    for dim, blocks in cuts:
        steps = jax.random.uniform(jax.random.fold_in(jax.random.fold_in(stream_key, 6), dim), (blocks,), jnp.float32, smallest / len(cuts), top_value / len(cuts))
        gain = gain * jnp.repeat(jnp.exp(steps), extent[dim] // blocks).reshape((-1,) + (1,) * (len(extent) - 1 - dim))
    return gain


def distinct(rng, rows, count, top, lift):
    order = jax.random.permutation(jax.random.fold_in(rng, 1), count)
    pull = order
    for power in range(3):
        pull = pull * pull // count
    pull = pull * lift // count
    lots = jax.random.randint(jax.random.fold_in(rng, 2), (rows, count), 0, 4096) + pull
    sure = jax.random.permutation(jax.random.fold_in(rng, 3), rows)[jnp.arange(count) % rows]
    lots = jnp.where(jnp.arange(rows)[:, None] == sure[None, :], 1 << 14, lots)
    score = lots * count + jnp.arange(count)
    return lax.top_k(score.astype(jnp.int32), top)[1].astype(jnp.int32)


def split_up(count, total, limit, slope):
    weights = [(1 << 20) // math.isqrt(standing ** slope) + 1 for standing in range(2, count + 1)]
    surplus, given = total - limit - (count - 1), [1] * (count - 1)
    while surplus > 0:
        movable = [i for i in range(count - 1) if given[i] < limit]
        whole, left = sum([weights[i] for i in movable]), surplus
        for i in movable:
            extra = min(limit - given[i], max(1, left * weights[i] // whole), surplus)
            given[i] = given[i] + extra
            surplus = surplus - extra
    return np.array([limit] + given)


def uneven_parts(stream_key, amount, total, limit, slope):
    if amount == 2:
        one = jax.random.randint(stream_key, (), max(1, total - limit), min(limit, total - 1) + 1)
        return jnp.stack([one, total - one])
    sizes = jnp.asarray(split_up(amount, total, limit, slope), jnp.int32)
    twos = (amount - 1) // 2
    source_of, taker = sizes[1:1 + 2 * twos:2], sizes[2:2 + 2 * twos:2]
    room = jnp.minimum(source_of - 1, limit - taker)
    passed = jax.random.randint(jax.random.fold_in(stream_key, 1), (twos,), 0, 1 << 20) % (room + 1)
    sizes = sizes.at[1:1 + 2 * twos:2].set(source_of - passed).at[2:2 + 2 * twos:2].set(taker + passed)
    return sizes[jax.random.permutation(jax.random.fold_in(stream_key, 2), amount)]


def normal_values(key, extent, spread, reach, shards=(), kind=jnp.bfloat16):
    array = spread * jax.random.normal(key, extent, jnp.float32)
    if shards:
        array = array * block_scale(key, extent, shards, -0.22, 0.18)
    return jnp.clip(array, -reach, reach).astype(kind)


def setup_inputs(seed: int = 0) -> dict:
    key_list = jax.random.split(jax.random.key(seed), 8)
    block_ids = distinct(key_list[0], UBLOCKS * N_ITEMS, N_USERS, PAIRS, 682).reshape((UBLOCKS, N_ITEMS, PAIRS))
    pair_live = jax.vmap(lambda own: uneven_parts(own, PAIRS, LIVE, NNZ, 2))(jax.random.split(key_list[1], UBLOCKS * N_ITEMS)).reshape((UBLOCKS, N_ITEMS, PAIRS)).astype(jnp.int32)
    user_rows = plant(jax.random.randint(key_list[2], (UBLOCKS, N_ITEMS, PAIRS, NNZ), 0, BLK), jax.random.fold_in(key_list[2], 1), 0, BLK - 1).astype(jnp.int32)
    item_rows = plant(jax.random.randint(key_list[3], (UBLOCKS, N_ITEMS, PAIRS, NNZ), 0, BLK), jax.random.fold_in(key_list[3], 1), 0, BLK - 1).astype(jnp.int32)
    counts = plant(jax.random.randint(key_list[4], (UBLOCKS, N_ITEMS, PAIRS, NNZ), 1, 9), jax.random.fold_in(key_list[4], 1), 1, 8).astype(jnp.int32)
    item_emb = draw_item_emb(jax.random.fold_in(key_list[7], 71), 0)
    user_emb = normal_values(key_list[6], (USERS, E), 1.0, 6.0, ((0, 192),), jnp.float32)
    return {"block_ids": block_ids, "pair_live": pair_live, "user_rows": user_rows, "item_rows": item_rows, "counts": counts, "item_emb": item_emb, "user_emb": user_emb}


conf_rate = 0.5
ridge_weight = 0.5


def reference(block_ids, pair_live, user_rows, item_rows, counts, item_emb, user_emb):
    highest = lax.Precision.HIGHEST
    rounded = lax.optimization_barrier(item_emb.astype(jnp.bfloat16))
    items_full = rounded.astype(jnp.float32)
    flat_items = items_full.reshape(N_ITEMS * IROWS, E)
    gramian = jnp.dot(flat_items.T, flat_items, precision=highest)
    base_matrix = gramian * (E / (N_ITEMS * IROWS)) + ridge_weight * jnp.eye(E, dtype=jnp.float32)
    item_blocks = items_full.reshape(N_ITEMS, N_USERS, BLK, E)
    shard_index = jnp.arange(N_ITEMS, dtype=jnp.int32)[:, None]
    slot_index = jnp.arange(NNZ, dtype=jnp.int32)
    row_index = jnp.arange(BLK, dtype=jnp.int32)

    def one_block(inputs_one):
        picked_ids, live_row, user_slot, item_slot, count_row, initial = inputs_one
        item_vecs = item_blocks[shard_index, picked_ids].reshape(N_ITEMS * PAIRS, BLK, E)
        live_mask = (slot_index[None, None, :] < live_row[:, :, None]).astype(jnp.float32)
        counts_float = count_row.astype(jnp.float32)
        confidence = (conf_rate * counts_float * live_mask).reshape(N_ITEMS * PAIRS, NNZ)
        full_conf = (live_mask * (1.0 + conf_rate * counts_float)).reshape(N_ITEMS * PAIRS, NNZ)
        onehot_user = (user_slot.reshape(N_ITEMS * PAIRS, NNZ)[:, :, None] == row_index).astype(jnp.float32)
        onehot_item = (item_slot.reshape(N_ITEMS * PAIRS, NNZ)[:, :, None] == row_index).astype(jnp.float32)
        weight_map = jnp.einsum('qkb,qki->qbi', onehot_user * confidence[:, :, None], onehot_item, precision=highest)
        weight_full = jnp.einsum('qkb,qki->qbi', onehot_user * full_conf[:, :, None], onehot_item, precision=highest)
        rhs = jnp.einsum('qbi,qie->be', weight_full, item_vecs, precision=highest)

        def operator(vectors):
            dot_table = jnp.einsum('be,qie->qbi', vectors, item_vecs, precision=highest)
            summed = jnp.einsum('qbi,qie->be', weight_map * dot_table, item_vecs, precision=highest)
            return jnp.dot(vectors, base_matrix, precision=highest) + summed

        solution = initial
        remain = rhs - operator(solution)
        direction = remain
        norm_now = jnp.sum(remain * remain, axis=1, keepdims=True)
        for turn_index in range(ITERS):
            image = operator(direction)
            step_len = norm_now / jnp.sum(direction * image, axis=1, keepdims=True)
            solution = solution + step_len * direction
            remain = remain - step_len * image
            norm_next = jnp.sum(remain * remain, axis=1, keepdims=True)
            direction = remain + (norm_next / norm_now) * direction
            norm_now = norm_next
        return solution

    starts = user_emb.reshape(UBLOCKS, BLK, E)
    solved = lax.map(one_block, (block_ids, pair_live, user_rows, item_rows, counts, starts))
    return solved.reshape(USERS, E)
```

```python
import functools

import jax
import jax.numpy as jnp
from jax import lax
from jax.experimental import pallas as pl
from jax.experimental.pallas import tpu as pltpu
from jax.sharding import Mesh, PartitionSpec as P

Z, Y, C, X = 12, 8, 2, 4
E = 128
BLK = 128
PAIRS = 8
NNZ = 64
LIVE = 320
ITERS = 3
GROUPS = 4
GRAM = E // (C * X)

conf_rate = 0.5
ridge_weight = 0.5

bf16 = jnp.bfloat16
f32 = jnp.float32


def dot(a, b):
    return lax.dot_general(a, b, (((1,), (0,)), ((), ())), preferred_element_type=f32)


def split(a):
    hi = a.astype(bf16)
    return hi, (a - hi.astype(f32)).astype(bf16)


def offsets(live_ref, base):
    out = [0]
    for p in range(PAIRS - 1):
        out.append(out[-1] + live_ref[base + p])
    return out


def weight_kernel(live_ref, user_ref, count_ref, out_ref, rows_ref):
    lane = lax.broadcasted_iota(jnp.int32, (NNZ, BLK), 1)
    slot = lax.broadcasted_iota(jnp.int32, (NNZ, BLK), 0)
    for s in range(X):
        offs = offsets(live_ref, s * PAIRS)
        for p in range(PAIRS):
            q = s * PAIRS + p
            hit = (user_ref[:, q : q + 1] == lane) & (slot < live_ref[q])
            rows = jnp.where(hit, count_ref[:, q : q + 1].astype(f32), 0.0)
            rows_ref[s, pl.ds(offs[p], NNZ), :] = rows
        out_ref[s * LIVE : (s + 1) * LIVE, :] = rows_ref[s, :LIVE, :].astype(bf16)


def select_kernel(
    block_ref, seen_ref, live_ref, item_ref, gram_ref, half_ref, out_ref, held, rows_ref, sems
):
    copies = []
    for q in range(C * GROUPS * PAIRS):
        start = pl.multiple_of(block_ref[q] * BLK, BLK)
        copy = pltpu.make_async_copy(half_ref.at[pl.ds(start, BLK), :], held.at[q], sems.at[q])
        copy.start()
        copies.append(copy)
    gram_hi, gram_lo = split(gram_ref[...])
    lane = lax.broadcasted_iota(jnp.int32, (NNZ, BLK), 1)
    slot = lax.broadcasted_iota(jnp.int32, (NNZ, BLK), 0)
    for d in range(C * GROUPS):
        offs = offsets(live_ref, d * PAIRS)
        for p in range(PAIRS):
            q = d * PAIRS + p
            hit = (item_ref[:, q : q + 1] == lane) & (slot < seen_ref[q])
            onehot = jnp.where(hit, 1.0, 0.0).astype(bf16)
            copies[q].wait()
            rows_ref[d, pl.ds(offs[p], NNZ), :] = dot(onehot, held[q])
        out_ref[d, :LIVE, :] = rows_ref[d, :LIVE, :].astype(bf16)
        out_ref[d, LIVE : LIVE + GRAM, :] = gram_hi
        out_ref[d, LIVE + GRAM :, :] = gram_lo


def solve_kernel(recv_ref, weight_ref, start_ref, out_ref):
    items = (recv_ref[:X, :LIVE, :] + recv_ref[X:, :LIVE, :]).reshape(X * LIVE, E)
    items_t = items.T
    weight = weight_ref[...]
    conf = weight.astype(f32) * conf_rate
    full = jnp.where(weight > 0, 1.0 + conf, 0.0).astype(bf16)
    gram = recv_ref[:, LIVE : LIVE + GRAM, :].astype(f32) + recv_ref[:, LIVE + GRAM :, :].astype(f32)
    gram = gram.reshape(E, E)
    eye = lax.broadcasted_iota(jnp.int32, (E, E), 0) == lax.broadcasted_iota(jnp.int32, (E, E), 1)
    base_hi, base_lo = split(
        gram * (E / (X * Z * Y * C * BLK)) + jnp.where(eye, ridge_weight, 0.0)
    )

    def operator(vectors):
        hi, lo = split(vectors)
        both = jnp.concatenate([hi, lo], axis=1)
        table = dot(items, both)
        table = conf * (table[:, :BLK] + table[:, BLK:])
        table_hi, table_lo = split(table)
        summed = dot(items_t, jnp.concatenate([table_hi, table_lo], axis=1))
        dense = dot(base_hi, both)
        return (
            (summed[:, :BLK] + summed[:, BLK:])
            + (dense[:, :BLK] + dense[:, BLK:])
            + dot(base_lo, hi)
        )

    x = start_ref[...].T
    remain = dot(items_t, full) - operator(x)
    direction = remain
    norm_now = jnp.sum(remain * remain, axis=0, keepdims=True)
    for turn in range(ITERS):
        image = operator(direction)
        step = norm_now / jnp.sum(direction * image, axis=0, keepdims=True)
        x = x + step * direction
        if turn < ITERS - 1:
            remain = remain - step * image
            norm_next = jnp.sum(remain * remain, axis=0, keepdims=True)
            direction = remain + norm_next / norm_now * direction
            norm_now = norm_next
    out_ref[...] = x.T


def vmem():
    return pl.BlockSpec(memory_space=pltpu.VMEM)


def smem():
    return pl.BlockSpec(memory_space=pltpu.SMEM)


def params():
    return pltpu.CompilerParams(vmem_limit_bytes=24 * 1024 * 1024)


def local(block_ids, pair_live, user_rows, item_rows, counts, item_emb, user_emb):
    core = lax.axis_index("core")
    part = lax.axis_index("x")
    own_block = item_emb[0].astype(bf16)
    with jax.named_scope("gather_z"):
        column = lax.all_gather(own_block, "z", axis=0, tiled=True)
    with jax.named_scope("gather_y"):
        half = lax.all_gather(column, "y", axis=0, tiled=True)

    with jax.named_scope("gramian"):
        gram = lax.dot_general(
            column, column, (((0,), (0,)), ((), ())), preferred_element_type=f32
        )
        gram = lax.all_to_all(gram.reshape(C * X, GRAM, E), ("core", "x"), 0, 0, tiled=True)
        gram = jnp.broadcast_to(jnp.sum(gram, axis=0)[None], (Y, GRAM, E))
        gram = jnp.sum(lax.all_to_all(gram, "y", 0, 0, tiled=True), axis=0)

    with jax.named_scope("index_exchange"):
        item_pack = jnp.concatenate(
            [
                item_rows.reshape(GROUPS, PAIRS * NNZ),
                jnp.pad(block_ids.reshape(GROUPS, PAIRS), ((0, 0), (0, NNZ - PAIRS))),
                jnp.pad(pair_live.reshape(GROUPS, PAIRS), ((0, 0), (0, NNZ - PAIRS))),
            ],
            axis=1,
        )
        item_pack = lax.all_gather(item_pack, "core", axis=0, tiled=False)
        item_pack = item_pack.reshape(C * GROUPS, (PAIRS + 2) * NNZ)
        user_pack = jnp.concatenate(
            [
                user_rows.reshape(GROUPS, PAIRS * NNZ),
                counts.reshape(GROUPS, PAIRS * NNZ),
                jnp.pad(pair_live.reshape(GROUPS, PAIRS), ((0, 0), (0, BLK - PAIRS))),
            ],
            axis=1,
        )
        user_pack = lax.all_to_all(user_pack, "x", 0, 0, tiled=True)

    span = PAIRS * NNZ
    ids = item_pack[:, span : span + PAIRS].reshape(-1)
    live = item_pack[:, span + NNZ : span + NNZ + PAIRS].reshape(-1)
    z_of, y_of, c_of = ids // (Y * C), ids // C % Y, ids % C
    spots = jnp.clip(y_of * Z + z_of, 0, Z * Y - 1)
    seen = jnp.where(c_of == core, live, 0)
    slots = item_pack[:, :span].reshape(C * GROUPS * PAIRS, NNZ).T

    with jax.named_scope("weights"):
        weight = pl.pallas_call(
            weight_kernel,
            out_shape=jax.ShapeDtypeStruct((X * LIVE, BLK), bf16),
            in_specs=[smem(), vmem(), vmem()],
            out_specs=vmem(),
            scratch_shapes=[pltpu.VMEM((X, LIVE + NNZ, BLK), f32)],
            compiler_params=params(),
            cost_estimate=pl.CostEstimate(flops=2_000_000, bytes_accessed=400_000, transcendentals=0),
        )(
            user_pack[:, 2 * span : 2 * span + PAIRS].reshape(-1),
            user_pack[:, :span].reshape(X * PAIRS, NNZ).T,
            user_pack[:, span : 2 * span].reshape(X * PAIRS, NNZ).T,
        )
    with jax.named_scope("select"):
        chosen = pl.pallas_call(
            select_kernel,
            out_shape=jax.ShapeDtypeStruct((C * GROUPS, LIVE + 2 * GRAM, E), bf16),
            in_specs=[smem()] * 3 + [vmem()] * 2 + [pl.BlockSpec(memory_space=pltpu.HBM)],
            out_specs=vmem(),
            scratch_shapes=[
                pltpu.VMEM((C * GROUPS * PAIRS, BLK, E), bf16),
                pltpu.VMEM((C * GROUPS, LIVE + NNZ, E), f32),
                pltpu.SemaphoreType.DMA((C * GROUPS * PAIRS,)),
            ],
            compiler_params=params(),
            cost_estimate=pl.CostEstimate(
                flops=140_000_000, bytes_accessed=3_000_000, transcendentals=0
            ),
        )(spots, seen, live, slots, gram, half)
    with jax.named_scope("exchange"):
        received = lax.all_to_all(chosen, ("core", "x"), 0, 0, tiled=True)
    with jax.named_scope("solve"):
        start = lax.dynamic_slice_in_dim(user_emb, part * BLK, BLK, 0)
        solved = pl.pallas_call(
            solve_kernel,
            out_shape=jax.ShapeDtypeStruct((BLK, E), f32),
            in_specs=[vmem()] * 3,
            out_specs=vmem(),
            compiler_params=params(),
            cost_estimate=pl.CostEstimate(
                flops=800_000_000, bytes_accessed=1_200_000, transcendentals=0
            ),
        )(received, weight, start)
    with jax.named_scope("gather_x"):
        return lax.all_gather(solved, "x", axis=0, tiled=True)


def solution(mesh):
    grid = Mesh(mesh.devices.reshape(Z, Y, C, X), ("z", "y", "core", "x"))
    users = ("z", "y", "core")
    return jax.shard_map(
        local,
        mesh=grid,
        in_specs=(
            P(users, "x", None),
            P(users, "x", None),
            P(users, "x", None, None),
            P(users, "x", None, None),
            P(users, "x", None, None),
            P("x", users, None),
            P(users, None),
        ),
        out_specs=P(users, None),
        check_vma=False,
    )
```

```python
import functools

import jax
import jax.numpy as jnp
from jax import lax
from jax.experimental import pallas as pl
from jax.experimental.pallas import tpu as pltpu
from jax.sharding import Mesh, PartitionSpec as P

Z, Y, C, X = 12, 8, 2, 4
E = 128
BLK = 128
PAIRS = 8
NNZ = 64
LIVE = 320
ITERS = 3
GROUPS = 4
GRAM = E // (C * X)

conf_rate = 0.5
ridge_weight = 0.5

bf16 = jnp.bfloat16
f32 = jnp.float32


def dot(a, b):
    return lax.dot_general(a, b, (((1,), (0,)), ((), ())), preferred_element_type=f32)


def split(a):
    hi = a.astype(bf16)
    return hi, (a - hi.astype(f32)).astype(bf16)


def offsets(live_ref, base):
    out = [0]
    for p in range(PAIRS - 1):
        out.append(out[-1] + live_ref[base + p])
    return out


def weight_kernel(live_ref, user_ref, count_ref, out_ref, rows_ref):
    lane = lax.broadcasted_iota(jnp.int32, (NNZ, BLK), 1)
    slot = lax.broadcasted_iota(jnp.int32, (NNZ, BLK), 0)
    for s in range(X):
        offs = offsets(live_ref, s * PAIRS)
        for p in range(PAIRS):
            q = s * PAIRS + p
            hit = (user_ref[:, q : q + 1] == lane) & (slot < live_ref[q])
            rows = jnp.where(hit, count_ref[:, q : q + 1].astype(f32), 0.0)
            rows_ref[s, pl.ds(offs[p], NNZ), :] = rows
        out_ref[s * LIVE : (s + 1) * LIVE, :] = rows_ref[s, :LIVE, :].astype(bf16)


def place_kernel(seen_ref, live_ref, item_ref, out_ref, rows_ref):
    lane = lax.broadcasted_iota(jnp.int32, (LIVE, BLK), 1)
    slot = lax.broadcasted_iota(jnp.int32, (NNZ, 1), 0)
    merged = jnp.full((LIVE, BLK), -1, jnp.int32)
    for d in range(C * GROUPS):
        offs = offsets(live_ref, d * PAIRS)
        for p in range(PAIRS):
            q = d * PAIRS + p
            spot = jnp.where(slot < seen_ref[q], item_ref[:, q : q + 1] + p * BLK, -1)
            rows_ref[d, pl.ds(offs[p], NNZ), :] = jnp.broadcast_to(spot, (NNZ, BLK))
        merged = jnp.where(lane == d, rows_ref[d, :LIVE, :], merged)
    out_ref[...] = merged


def select_kernel(block_ref, place_ref, gram_ref, half_ref, out_ref):
    gram_hi, gram_lo = split(gram_ref[...])
    lane = lax.broadcasted_iota(jnp.int32, (LIVE, PAIRS * BLK), 1)
    for d in range(C * GROUPS):
        blocks = []
        for p in range(PAIRS):
            start = pl.multiple_of(block_ref[d * PAIRS + p] * BLK, BLK)
            blocks.append(half_ref[pl.ds(start, BLK), :])
        onehot = jnp.where(place_ref[:, d : d + 1] == lane, 1.0, 0.0).astype(bf16)
        rows = dot(onehot, jnp.concatenate(blocks, axis=0))
        out_ref[d, :LIVE, :] = rows.astype(bf16)
        out_ref[d, LIVE : LIVE + GRAM, :] = gram_hi
        out_ref[d, LIVE + GRAM :, :] = gram_lo


def solve_kernel(recv_ref, weight_ref, start_ref, out_ref):
    items = (recv_ref[:X, :LIVE, :] + recv_ref[X:, :LIVE, :]).reshape(X * LIVE, E)
    items_t = items.T
    weight = weight_ref[...]
    conf = weight.astype(f32) * conf_rate
    full = jnp.where(weight > 0, 1.0 + conf, 0.0).astype(bf16)
    gram = recv_ref[:, LIVE : LIVE + GRAM, :].astype(f32) + recv_ref[:, LIVE + GRAM :, :].astype(f32)
    gram = gram.reshape(E, E)
    eye = lax.broadcasted_iota(jnp.int32, (E, E), 0) == lax.broadcasted_iota(jnp.int32, (E, E), 1)
    base_hi, base_lo = split(
        gram * (E / (X * Z * Y * C * BLK)) + jnp.where(eye, ridge_weight, 0.0)
    )

    def operator(vectors):
        hi, lo = split(vectors)
        both = jnp.concatenate([hi, lo], axis=1)
        table = dot(items, both)
        table = conf * (table[:, :BLK] + table[:, BLK:])
        table_hi, table_lo = split(table)
        summed = dot(items_t, jnp.concatenate([table_hi, table_lo], axis=1))
        dense = dot(base_hi, both)
        return (
            (summed[:, :BLK] + summed[:, BLK:])
            + (dense[:, :BLK] + dense[:, BLK:])
            + dot(base_lo, hi)
        )

    x = start_ref[...].T
    remain = dot(items_t, full) - operator(x)
    direction = remain
    norm_now = jnp.sum(remain * remain, axis=0, keepdims=True)
    for turn in range(ITERS):
        image = operator(direction)
        step = norm_now / jnp.sum(direction * image, axis=0, keepdims=True)
        x = x + step * direction
        if turn < ITERS - 1:
            remain = remain - step * image
            norm_next = jnp.sum(remain * remain, axis=0, keepdims=True)
            direction = remain + norm_next / norm_now * direction
            norm_now = norm_next
    out_ref[...] = x.T


def vmem():
    return pl.BlockSpec(memory_space=pltpu.VMEM)


def smem():
    return pl.BlockSpec(memory_space=pltpu.SMEM)


def params():
    return pltpu.CompilerParams(vmem_limit_bytes=24 * 1024 * 1024)


def local(block_ids, pair_live, user_rows, item_rows, counts, item_emb, user_emb):
    core = lax.axis_index("core")
    part = lax.axis_index("x")
    own_block = item_emb[0].astype(bf16)
    with jax.named_scope("gather_z"):
        column = lax.all_gather(own_block, "z", axis=0, tiled=True)
    with jax.named_scope("gather_y"):
        half = lax.all_gather(column, "y", axis=0, tiled=True)

    with jax.named_scope("gramian"):
        gram = lax.dot_general(
            column, column, (((0,), (0,)), ((), ())), preferred_element_type=f32
        )
        gram = lax.all_to_all(gram.reshape(C * X, GRAM, E), ("core", "x"), 0, 0, tiled=True)
        gram = jnp.broadcast_to(jnp.sum(gram, axis=0)[None], (Y, GRAM, E))
        gram = jnp.sum(lax.all_to_all(gram, "y", 0, 0, tiled=True), axis=0)

    with jax.named_scope("index_exchange"):
        item_pack = jnp.concatenate(
            [
                item_rows.reshape(GROUPS, PAIRS * NNZ),
                jnp.pad(block_ids.reshape(GROUPS, PAIRS), ((0, 0), (0, NNZ - PAIRS))),
                jnp.pad(pair_live.reshape(GROUPS, PAIRS), ((0, 0), (0, NNZ - PAIRS))),
            ],
            axis=1,
        )
        item_pack = lax.all_gather(item_pack, "core", axis=0, tiled=False)
        item_pack = item_pack.reshape(C * GROUPS, (PAIRS + 2) * NNZ)
        user_pack = jnp.concatenate(
            [
                user_rows.reshape(GROUPS, PAIRS * NNZ),
                counts.reshape(GROUPS, PAIRS * NNZ),
                jnp.pad(pair_live.reshape(GROUPS, PAIRS), ((0, 0), (0, BLK - PAIRS))),
            ],
            axis=1,
        )
        user_pack = lax.all_to_all(user_pack, "x", 0, 0, tiled=True)

    span = PAIRS * NNZ
    ids = item_pack[:, span : span + PAIRS].reshape(-1)
    live = item_pack[:, span + NNZ : span + NNZ + PAIRS].reshape(-1)
    z_of, y_of, c_of = ids // (Y * C), ids // C % Y, ids % C
    spots = jnp.clip(y_of * Z + z_of, 0, Z * Y - 1)
    seen = jnp.where(c_of == core, live, 0)
    slots = item_pack[:, :span].reshape(C * GROUPS * PAIRS, NNZ).T

    with jax.named_scope("weights"):
        weight = pl.pallas_call(
            weight_kernel,
            out_shape=jax.ShapeDtypeStruct((X * LIVE, BLK), bf16),
            in_specs=[smem(), vmem(), vmem()],
            out_specs=vmem(),
            scratch_shapes=[pltpu.VMEM((X, LIVE + NNZ, BLK), f32)],
            compiler_params=params(),
            cost_estimate=pl.CostEstimate(flops=2_000_000, bytes_accessed=400_000, transcendentals=0),
        )(
            user_pack[:, 2 * span : 2 * span + PAIRS].reshape(-1),
            user_pack[:, :span].reshape(X * PAIRS, NNZ).T,
            user_pack[:, span : 2 * span].reshape(X * PAIRS, NNZ).T,
        )
    with jax.named_scope("place"):
        place = pl.pallas_call(
            place_kernel,
            out_shape=jax.ShapeDtypeStruct((LIVE, BLK), jnp.int32),
            in_specs=[smem(), smem(), vmem()],
            out_specs=vmem(),
            scratch_shapes=[pltpu.VMEM((C * GROUPS, LIVE + NNZ, BLK), jnp.int32)],
            compiler_params=params(),
            cost_estimate=pl.CostEstimate(
                flops=2_000_000, bytes_accessed=300_000, transcendentals=0
            ),
        )(seen, live, slots)
    with jax.named_scope("select"):
        chosen = pl.pallas_call(
            select_kernel,
            out_shape=jax.ShapeDtypeStruct((C * GROUPS, LIVE + 2 * GRAM, E), bf16),
            in_specs=[smem()] + [vmem()] * 3,
            out_specs=vmem(),
            compiler_params=params(),
            cost_estimate=pl.CostEstimate(
                flops=700_000_000, bytes_accessed=4_000_000, transcendentals=0
            ),
        )(spots, place, gram, half)
    with jax.named_scope("exchange"):
        received = lax.all_to_all(chosen, ("core", "x"), 0, 0, tiled=True)
    with jax.named_scope("solve"):
        start = lax.dynamic_slice_in_dim(user_emb, part * BLK, BLK, 0)
        solved = pl.pallas_call(
            solve_kernel,
            out_shape=jax.ShapeDtypeStruct((BLK, E), f32),
            in_specs=[vmem()] * 3,
            out_specs=vmem(),
            compiler_params=params(),
            cost_estimate=pl.CostEstimate(
                flops=800_000_000, bytes_accessed=1_200_000, transcendentals=0
            ),
        )(received, weight, start)
    with jax.named_scope("gather_x"):
        return lax.all_gather(solved, "x", axis=0, tiled=True)


def solution(mesh):
    grid = Mesh(mesh.devices.reshape(Z, Y, C, X), ("z", "y", "core", "x"))
    users = ("z", "y", "core")
    return jax.shard_map(
        local,
        mesh=grid,
        in_specs=(
            P(users, "x", None),
            P(users, "x", None),
            P(users, "x", None, None),
            P(users, "x", None, None),
            P(users, "x", None, None),
            P("x", users, None),
            P(users, None),
        ),
        out_specs=P(users, None),
        check_vma=False,
    )
```

```python
import functools

import jax
import jax.numpy as jnp
from jax import lax
from jax.experimental import pallas as pl
from jax.experimental.pallas import tpu as pltpu
from jax.sharding import Mesh, PartitionSpec as P

Z, Y, C, X = 12, 8, 2, 4
E = 128
BLK = 128
PAIRS = 8
NNZ = 64
LIVE = 320
ITERS = 3
GROUPS = 4
GRAM = E // (C * X)

conf_rate = 0.5
ridge_weight = 0.5

bf16 = jnp.bfloat16
f32 = jnp.float32


def dot(a, b):
    return lax.dot_general(a, b, (((1,), (0,)), ((), ())), preferred_element_type=f32)


def split(a):
    hi = a.astype(bf16)
    return hi, (a - hi.astype(f32)).astype(bf16)


def offsets(live_ref, base):
    out = [0]
    for p in range(PAIRS - 1):
        out.append(out[-1] + live_ref[base + p])
    return out


def weight_kernel(live_ref, user_ref, count_ref, out_ref, rows_ref):
    lane = lax.broadcasted_iota(jnp.int32, (NNZ, BLK), 1)
    slot = lax.broadcasted_iota(jnp.int32, (NNZ, BLK), 0)
    for s in range(X):
        offs = offsets(live_ref, s * PAIRS)
        for p in range(PAIRS):
            q = s * PAIRS + p
            hit = (user_ref[:, q : q + 1] == lane) & (slot < live_ref[q])
            rows = jnp.where(hit, count_ref[:, q : q + 1].astype(f32), 0.0)
            rows_ref[s, pl.ds(offs[p], NNZ), :] = rows
        out_ref[s * LIVE : (s + 1) * LIVE, :] = rows_ref[s, :LIVE, :].astype(bf16)


def place_kernel(seen_ref, live_ref, item_ref, out_ref, rows_ref):
    lane = lax.broadcasted_iota(jnp.int32, (LIVE, BLK), 1)
    slot = lax.broadcasted_iota(jnp.int32, (NNZ, 1), 0)
    merged = jnp.full((LIVE, BLK), -1, jnp.int32)
    for d in range(C * GROUPS):
        offs = offsets(live_ref, d * PAIRS)
        for p in range(PAIRS):
            q = d * PAIRS + p
            spot = jnp.where(slot < seen_ref[q], item_ref[:, q : q + 1] + p * BLK, -1)
            rows_ref[d, pl.ds(offs[p], NNZ), :] = jnp.broadcast_to(spot, (NNZ, BLK))
        merged = jnp.where(lane == d, rows_ref[d, :LIVE, :], merged)
    out_ref[...] = merged


def select_kernel(block_ref, place_ref, gram_ref, half_ref, out_ref):
    gram_hi, gram_lo = split(gram_ref[...])
    lane = lax.broadcasted_iota(jnp.int32, (LIVE, PAIRS * BLK), 1)
    for d in range(C * GROUPS):
        blocks = []
        for p in range(PAIRS):
            start = pl.multiple_of(block_ref[d * PAIRS + p] * BLK, BLK)
            blocks.append(half_ref[pl.ds(start, BLK), :])
        onehot = jnp.where(place_ref[:, d : d + 1] == lane, 1.0, 0.0).astype(bf16)
        rows = dot(onehot, jnp.concatenate(blocks, axis=0))
        out_ref[d, :LIVE, :] = rows.astype(bf16)
        out_ref[d, LIVE : LIVE + GRAM, :] = gram_hi
        out_ref[d, LIVE + GRAM :, :] = gram_lo


def solve_kernel(recv_ref, weight_ref, start_ref, out_ref):
    items = (recv_ref[:X, :LIVE, :] + recv_ref[X:, :LIVE, :]).reshape(X * LIVE, E)
    items_t = items.T
    weight = weight_ref[...]
    conf = weight.astype(f32) * conf_rate
    full = jnp.where(weight > 0, 1.0 + conf, 0.0).astype(bf16)
    gram = recv_ref[:, LIVE : LIVE + GRAM, :].astype(f32) + recv_ref[:, LIVE + GRAM :, :].astype(f32)
    gram = gram.reshape(E, E)
    eye = lax.broadcasted_iota(jnp.int32, (E, E), 0) == lax.broadcasted_iota(jnp.int32, (E, E), 1)
    base_hi, base_lo = split(
        gram * (E / (X * Z * Y * C * BLK)) + jnp.where(eye, ridge_weight, 0.0)
    )

    def operator(vectors):
        hi, lo = split(vectors)
        both = jnp.concatenate([hi, lo], axis=1)
        table = dot(items, both)
        table = conf * (table[:, :BLK] + table[:, BLK:])
        table_hi, table_lo = split(table)
        summed = dot(items_t, jnp.concatenate([table_hi, table_lo], axis=1))
        dense = dot(base_hi, both)
        return (
            (summed[:, :BLK] + summed[:, BLK:])
            + (dense[:, :BLK] + dense[:, BLK:])
            + dot(base_lo, hi)
        )

    x = start_ref[...].T
    remain = dot(items_t, full) - operator(x)
    direction = remain
    norm_now = jnp.sum(remain * remain, axis=0, keepdims=True)
    for turn in range(ITERS):
        image = operator(direction)
        step = norm_now / jnp.sum(direction * image, axis=0, keepdims=True)
        x = x + step * direction
        if turn < ITERS - 1:
            remain = remain - step * image
            norm_next = jnp.sum(remain * remain, axis=0, keepdims=True)
            direction = remain + norm_next / norm_now * direction
            norm_now = norm_next
    out_ref[...] = x.T


def vmem():
    return pl.BlockSpec(memory_space=pltpu.VMEM)


def smem():
    return pl.BlockSpec(memory_space=pltpu.SMEM)


def params():
    return pltpu.CompilerParams(vmem_limit_bytes=24 * 1024 * 1024)


def spread(value, axis, size):
    return lax.all_to_all(jnp.broadcast_to(value[None], (size,) + value.shape), axis, 0, 0, tiled=True)


def from_next(value):
    return lax.ppermute(value, "y", [(i, (i - 1) % Y) for i in range(Y)])


def from_last(value):
    return lax.ppermute(value, "y", [(i, (i + 1) % Y) for i in range(Y)])


def lines(values, width):
    rows = values.reshape(-1, width).astype(f32)
    return jnp.pad(rows, ((0, 0), (0, BLK - width)))


def local(block_ids, pair_live, user_rows, item_rows, counts, item_emb, user_emb):
    core = lax.axis_index("core")
    part = lax.axis_index("x")
    own_block = item_emb[0].astype(bf16)
    with jax.named_scope("gather_z"):
        column = lax.all_gather(own_block, "z", axis=0, tiled=True)
    with jax.named_scope("gather_y"):
        ups, downs = [column], [column]
        for _ in range(Y // 2 - 1):
            ups.append(from_next(ups[-1]))
            downs.append(from_last(downs[-1]))
        ups.append(from_next(ups[-1]))
        half = jnp.concatenate(ups + downs[:0:-1], axis=0)

    with jax.named_scope("gramian"):
        gram = lax.dot_general(
            column, column, (((0,), (0,)), ((), ())), preferred_element_type=f32
        ).reshape(C * X, GRAM, E)
    with jax.named_scope("index_exchange"):
        user_pack = jnp.concatenate(
            [
                lines(user_rows, BLK).reshape(GROUPS, -1, BLK),
                lines(counts, BLK).reshape(GROUPS, -1, BLK),
                lines(pair_live, PAIRS).reshape(GROUPS, -1, BLK),
            ],
            axis=1,
        )
        item_pack = jnp.concatenate(
            [
                lines(item_rows, BLK),
                lines(block_ids, GROUPS * PAIRS),
                lines(pair_live, GROUPS * PAIRS),
            ],
            axis=0,
        )
        pack = jnp.concatenate(
            [
                gram,
                jnp.tile(user_pack, (C, 1, 1)),
                jnp.broadcast_to(item_pack[None], (C * X,) + item_pack.shape),
            ],
            axis=1,
        )
        n_user, n_item = user_pack.shape[1], item_pack.shape[0]
        pack = jnp.pad(pack, ((0, 0), (0, -pack.shape[1] % 8), (0, 0)))
        pack = lax.all_to_all(pack, ("core", "x"), 0, 0, tiled=True)
        gram = jnp.sum(pack[:, :GRAM], axis=0)
        pack = pack.reshape(C, X, -1, BLK)
        user_pack = lax.dynamic_index_in_dim(pack, core, 0, keepdims=False)
        user_pack = user_pack[:, GRAM : GRAM + n_user].astype(jnp.int32)
        item_pack = lax.dynamic_index_in_dim(pack, part, 1, keepdims=False)
        item_pack = item_pack[:, GRAM + n_user : GRAM + n_user + n_item].astype(jnp.int32)
    with jax.named_scope("gramian"):
        gram = jnp.sum(spread(gram, "y", Y), axis=0)

    span = PAIRS * NNZ // BLK
    ids = item_pack[:, -2, : GROUPS * PAIRS].reshape(-1)
    live = item_pack[:, -1, : GROUPS * PAIRS].reshape(-1)
    z_of, y_of, c_of = ids // (Y * C), ids // C % Y, ids % C
    turn = (y_of - lax.axis_index("y")) % Y
    spots = jnp.clip(turn * Z + z_of, 0, Z * Y - 1)
    seen = jnp.where(c_of == core, live, 0)
    slots = item_pack[:, :-2].reshape(C * GROUPS * PAIRS, NNZ).T

    with jax.named_scope("weights"):
        weight = pl.pallas_call(
            weight_kernel,
            out_shape=jax.ShapeDtypeStruct((X * LIVE, BLK), bf16),
            in_specs=[smem(), vmem(), vmem()],
            out_specs=vmem(),
            scratch_shapes=[pltpu.VMEM((X, LIVE + NNZ, BLK), f32)],
            compiler_params=params(),
            cost_estimate=pl.CostEstimate(flops=2_000_000, bytes_accessed=400_000, transcendentals=0),
        )(
            user_pack[:, 2 * span, :PAIRS].reshape(-1),
            user_pack[:, :span].reshape(X * PAIRS, NNZ).T,
            user_pack[:, span : 2 * span].reshape(X * PAIRS, NNZ).T,
        )
    with jax.named_scope("place"):
        place = pl.pallas_call(
            place_kernel,
            out_shape=jax.ShapeDtypeStruct((LIVE, BLK), jnp.int32),
            in_specs=[smem(), smem(), vmem()],
            out_specs=vmem(),
            scratch_shapes=[pltpu.VMEM((C * GROUPS, LIVE + NNZ, BLK), jnp.int32)],
            compiler_params=params(),
            cost_estimate=pl.CostEstimate(
                flops=2_000_000, bytes_accessed=300_000, transcendentals=0
            ),
        )(seen, live, slots)
    with jax.named_scope("select"):
        chosen = pl.pallas_call(
            select_kernel,
            out_shape=jax.ShapeDtypeStruct((C * GROUPS, LIVE + 2 * GRAM, E), bf16),
            in_specs=[smem()] + [vmem()] * 3,
            out_specs=vmem(),
            compiler_params=params(),
            cost_estimate=pl.CostEstimate(
                flops=700_000_000, bytes_accessed=4_000_000, transcendentals=0
            ),
        )(spots, place, gram, half)
    with jax.named_scope("exchange"):
        received = lax.all_to_all(chosen, ("core", "x"), 0, 0, tiled=True)
    with jax.named_scope("solve"):
        start = lax.dynamic_slice_in_dim(user_emb, part * BLK, BLK, 0)
        solved = pl.pallas_call(
            solve_kernel,
            out_shape=jax.ShapeDtypeStruct((BLK, E), f32),
            in_specs=[vmem()] * 3,
            out_specs=vmem(),
            compiler_params=params(),
            cost_estimate=pl.CostEstimate(
                flops=800_000_000, bytes_accessed=1_200_000, transcendentals=0
            ),
        )(received, weight, start)
    with jax.named_scope("gather_x"):
        return spread(solved, "x", X).reshape(X * BLK, E)


def solution(mesh):
    grid = Mesh(mesh.devices.reshape(Z, Y, C, X), ("z", "y", "core", "x"))
    users = ("z", "y", "core")
    return jax.shard_map(
        local,
        mesh=grid,
        in_specs=(
            P(users, "x", None),
            P(users, "x", None),
            P(users, "x", None, None),
            P(users, "x", None, None),
            P(users, "x", None, None),
            P("x", users, None),
            P(users, None),
        ),
        out_specs=P(users, None),
        check_vma=False,
    )
```

```python
import functools

import jax
import jax.numpy as jnp
from jax import lax
from jax.experimental import pallas as pl
from jax.experimental.pallas import tpu as pltpu
from jax.sharding import Mesh, PartitionSpec as P

Z, Y, C, X = 12, 8, 2, 4
E = 128
BLK = 128
PAIRS = 8
NNZ = 64
LIVE = 320
ITERS = 3
GROUPS = 4
GRAM = E // (C * X)

conf_rate = 0.5
ridge_weight = 0.5

bf16 = jnp.bfloat16
f32 = jnp.float32


def dot(a, b):
    return lax.dot_general(a, b, (((1,), (0,)), ((), ())), preferred_element_type=f32)


def split(a):
    hi = a.astype(bf16)
    return hi, (a - hi.astype(f32)).astype(bf16)


def offsets(live_ref, base):
    out = [0]
    for p in range(PAIRS - 1):
        out.append(out[-1] + live_ref[base + p])
    return out


USER_AT = GRAM
COUNT_AT = USER_AT + PAIRS
ITEM_AT = COUNT_AT + PAIRS
BLOCK_AT = ITEM_AT + GROUPS * PAIRS
LIVE_AT = BLOCK_AT + GROUPS
PACK = LIVE_AT + GROUPS


def pack_kernel(gram_ref, block_ref, live_ref, user_ref, item_ref, count_ref, out_ref):
    out_ref[...] = jnp.zeros(out_ref.shape, f32)
    items = item_ref[...].reshape(GROUPS * PAIRS, NNZ).astype(f32)
    for d in range(C * X):
        out_ref[d, :GRAM, :] = gram_ref[d * GRAM : (d + 1) * GRAM, :]
        out_ref[d, USER_AT : USER_AT + PAIRS, :NNZ] = user_ref[d % X].astype(f32)
        out_ref[d, COUNT_AT : COUNT_AT + PAIRS, :NNZ] = count_ref[d % X].astype(f32)
        out_ref[d, ITEM_AT : ITEM_AT + GROUPS * PAIRS, :NNZ] = items
        out_ref[d, BLOCK_AT : BLOCK_AT + GROUPS, :PAIRS] = block_ref[...].astype(f32)
        out_ref[d, LIVE_AT : LIVE_AT + GROUPS, :PAIRS] = live_ref[...].astype(f32)


def weight_kernel(core_ref, live_ref, pack_ref, out_ref, rows_ref):
    packs = [pack_ref[core_ref[0] * X + s] for s in range(X)]
    users = [pack[USER_AT : USER_AT + PAIRS] for pack in packs]
    counts = [pack[COUNT_AT : COUNT_AT + PAIRS] for pack in packs]
    table = jnp.concatenate(users + counts, axis=0).T[:NNZ]
    lane = lax.broadcasted_iota(jnp.int32, (NNZ, BLK), 1).astype(f32)
    slot = lax.broadcasted_iota(jnp.int32, (NNZ, BLK), 0)
    for s in range(X):
        offs = offsets(live_ref, s * PAIRS)
        for p in range(PAIRS):
            q = s * PAIRS + p
            hit = (table[:, q : q + 1] == lane) & (slot < live_ref[q])
            rows = jnp.where(hit, table[:, X * PAIRS + q : X * PAIRS + q + 1], 0.0)
            rows_ref[s, pl.ds(offs[p], NNZ), :] = rows
        out_ref[s * LIVE : (s + 1) * LIVE, :] = rows_ref[s, :LIVE, :].astype(bf16)


def place_kernel(part_ref, seen_ref, live_ref, pack_ref, out_ref, rows_ref):
    items = [
        pack_ref[c * X + part_ref[0], ITEM_AT : ITEM_AT + GROUPS * PAIRS, :] for c in range(C)
    ]
    table = jnp.concatenate(items, axis=0).T[:NNZ].astype(jnp.int32)
    lane = lax.broadcasted_iota(jnp.int32, (LIVE, BLK), 1)
    slot = lax.broadcasted_iota(jnp.int32, (NNZ, 1), 0)
    merged = jnp.full((LIVE, BLK), -1, jnp.int32)
    for d in range(C * GROUPS):
        offs = offsets(live_ref, d * PAIRS)
        for p in range(PAIRS):
            q = d * PAIRS + p
            spot = jnp.where(slot < seen_ref[q], table[:, q : q + 1] + p * BLK, -1)
            rows_ref[d, pl.ds(offs[p], NNZ), :] = jnp.broadcast_to(spot, (NNZ, BLK))
        merged = jnp.where(lane == d, rows_ref[d, :LIVE, :], merged)
    out_ref[...] = merged


def select_kernel(turn_ref, block_ref, place_ref, gram_ref, *refs):
    piece_refs, out_ref = refs[:-1], refs[-1]
    gram_hi, gram_lo = split(gram_ref[...])
    lane = lax.broadcasted_iota(jnp.int32, (LIVE, PAIRS * BLK), 1)
    for d in range(C * GROUPS):
        blocks = []
        for p in range(PAIRS):
            q = d * PAIRS + p
            turn, spot = turn_ref[q], block_ref[q]
            block = piece_refs[0][spot]
            for t in range(1, Y):
                block = jnp.where(turn == t, piece_refs[t][spot], block)
            blocks.append(block)
        onehot = jnp.where(place_ref[:, d : d + 1] == lane, 1.0, 0.0).astype(bf16)
        rows = dot(onehot, jnp.concatenate(blocks, axis=0))
        out_ref[d, :LIVE, :] = rows.astype(bf16)
        out_ref[d, LIVE : LIVE + GRAM, :] = gram_hi
        out_ref[d, LIVE + GRAM :, :] = gram_lo


def solve_kernel(recv_ref, weight_ref, start_ref, out_ref):
    items = (recv_ref[:X, :LIVE, :] + recv_ref[X:, :LIVE, :]).reshape(X * LIVE, E)
    items_t = items.T
    weight = weight_ref[...]
    conf = weight.astype(f32) * conf_rate
    full = jnp.where(weight > 0, 1.0 + conf, 0.0).astype(bf16)
    gram = recv_ref[:, LIVE : LIVE + GRAM, :].astype(f32) + recv_ref[:, LIVE + GRAM :, :].astype(f32)
    gram = gram.reshape(E, E)
    eye = lax.broadcasted_iota(jnp.int32, (E, E), 0) == lax.broadcasted_iota(jnp.int32, (E, E), 1)
    base_hi, base_lo = split(
        gram * (E / (X * Z * Y * C * BLK)) + jnp.where(eye, ridge_weight, 0.0)
    )

    def operator(vectors):
        hi, lo = split(vectors)
        both = jnp.concatenate([hi, lo], axis=1)
        table = dot(items, both)
        table = conf * (table[:, :BLK] + table[:, BLK:])
        table_hi, table_lo = split(table)
        summed = dot(items_t, jnp.concatenate([table_hi, table_lo], axis=1))
        dense = dot(base_hi, both)
        return (
            (summed[:, :BLK] + summed[:, BLK:])
            + (dense[:, :BLK] + dense[:, BLK:])
            + dot(base_lo, hi)
        )

    x = start_ref[...].T
    remain = dot(items_t, full) - operator(x)
    direction = remain
    norm_now = jnp.sum(remain * remain, axis=0, keepdims=True)
    for turn in range(ITERS):
        image = operator(direction)
        step = norm_now / jnp.sum(direction * image, axis=0, keepdims=True)
        x = x + step * direction
        if turn < ITERS - 1:
            remain = remain - step * image
            norm_next = jnp.sum(remain * remain, axis=0, keepdims=True)
            direction = remain + norm_next / norm_now * direction
            norm_now = norm_next
    out_ref[...] = x.T


def vmem():
    return pl.BlockSpec(memory_space=pltpu.VMEM)


def smem():
    return pl.BlockSpec(memory_space=pltpu.SMEM)


def spread(value, axis, size):
    return lax.all_to_all(jnp.broadcast_to(value[None], (size,) + value.shape), axis, 0, 0, tiled=True)


def from_next(value):
    return lax.ppermute(value, "y", [(i, (i - 1) % Y) for i in range(Y)])


def from_last(value):
    return lax.ppermute(value, "y", [(i, (i + 1) % Y) for i in range(Y)])


def call(kernel, out, ins, scratch=(), flops=1_000_000, nbytes=400_000):
    return pl.pallas_call(
        kernel,
        out_shape=out,
        in_specs=ins,
        out_specs=vmem(),
        scratch_shapes=list(scratch),
        compiler_params=pltpu.CompilerParams(vmem_limit_bytes=24 * 1024 * 1024),
        cost_estimate=pl.CostEstimate(flops=flops, bytes_accessed=nbytes, transcendentals=0),
    )


def local(block_ids, pair_live, user_rows, item_rows, counts, item_emb, user_emb):
    core = lax.axis_index("core")
    part = lax.axis_index("x")
    own_block = item_emb[0].astype(bf16)
    with jax.named_scope("gather_z"):
        column = lax.all_gather(own_block, "z", axis=0, tiled=True)
    with jax.named_scope("gather_y"):
        ups, downs = [column], [column]
        for _ in range(Y // 2 - 1):
            ups.append(from_next(ups[-1]))
            downs.append(from_last(downs[-1]))
        ups.append(from_next(ups[-1]))
        pieces = [piece.reshape(Z, BLK, E) for piece in ups + downs[:0:-1]]

    with jax.named_scope("gramian"):
        gram = lax.dot_general(
            column, column, (((0,), (0,)), ((), ())), preferred_element_type=f32
        )
    with jax.named_scope("small_exchange"):
        pack = call(
            pack_kernel, jax.ShapeDtypeStruct((C * X, PACK, BLK), f32), [vmem()] * 6
        )(
            gram,
            block_ids[:, 0],
            pair_live[:, 0],
            user_rows[:, 0],
            item_rows[:, 0],
            counts[:, 0],
        )
        pack, _ = lax.optimization_barrier((pack, ups[1]))
        pack = lax.all_to_all(pack, ("core", "x"), 0, 0, tiled=True)
    with jax.named_scope("gramian"):
        gram = jnp.sum(spread(jnp.sum(pack[:, :GRAM], axis=0), "y", Y), axis=0)

    with jax.named_scope("indices"):
        grid = pack.reshape(C, X, PACK, BLK)
        own = lax.dynamic_slice(grid, (0, part, BLOCK_AT, 0), (C, 1, 2 * GROUPS, PAIRS))
        own = own.reshape(C, 2 * GROUPS, PAIRS).astype(jnp.int32)
        ids, live = own[:, :GROUPS].reshape(-1), own[:, GROUPS:].reshape(-1)
        z_of, y_of, c_of = ids // (Y * C), ids // C % Y, ids % C
        turns = (y_of - lax.axis_index("y")) % Y
        spots = jnp.clip(z_of, 0, Z - 1)
        seen = jnp.where(c_of == core, live, 0)
        user_live = lax.dynamic_slice(grid, (core, 0, LIVE_AT + part, 0), (1, X, 1, PAIRS))
        user_live = user_live.reshape(-1).astype(jnp.int32)

    with jax.named_scope("place"):
        place = call(
            place_kernel,
            jax.ShapeDtypeStruct((LIVE, BLK), jnp.int32),
            [smem()] * 3 + [vmem()],
            [pltpu.VMEM((C * GROUPS, LIVE + NNZ, BLK), jnp.int32)],
        )(part.reshape(1), seen, live, pack)
    with jax.named_scope("weights"):
        weight = call(
            weight_kernel,
            jax.ShapeDtypeStruct((X * LIVE, BLK), bf16),
            [smem()] * 2 + [vmem()],
            [pltpu.VMEM((X, LIVE + NNZ, BLK), f32)],
        )(core.reshape(1), user_live, pack)
    with jax.named_scope("select"):
        chosen = call(
            select_kernel,
            jax.ShapeDtypeStruct((C * GROUPS, LIVE + 2 * GRAM, E), bf16),
            [smem()] * 2 + [vmem()] * (2 + len(pieces)),
            flops=700_000_000,
            nbytes=4_000_000,
        )(turns, spots, place, gram, *pieces)
    with jax.named_scope("exchange"):
        received = lax.all_to_all(chosen, ("core", "x"), 0, 0, tiled=True)
    with jax.named_scope("solve"):
        start = lax.dynamic_slice_in_dim(user_emb, part * BLK, BLK, 0)
        solved = call(
            solve_kernel,
            jax.ShapeDtypeStruct((BLK, E), f32),
            [vmem()] * 3,
            flops=800_000_000,
            nbytes=1_200_000,
        )(received, weight, start)
    with jax.named_scope("gather_x"):
        return spread(solved, "x", X).reshape(X * BLK, E)


def solution(mesh):
    grid = Mesh(mesh.devices.reshape(Z, Y, C, X), ("z", "y", "core", "x"))
    users = ("z", "y", "core")
    return jax.shard_map(
        local,
        mesh=grid,
        in_specs=(
            P(users, "x", None),
            P(users, "x", None),
            P(users, "x", None, None),
            P(users, "x", None, None),
            P(users, "x", None, None),
            P("x", users, None),
            P(users, None),
        ),
        out_specs=P(users, None),
        check_vma=False,
    )
```

```python
import functools

import jax
import jax.numpy as jnp
from jax import lax
from jax.experimental import pallas as pl
from jax.experimental.pallas import tpu as pltpu
from jax.sharding import Mesh, PartitionSpec as P

Z, Y, C, X = 12, 8, 2, 4
E = 128
BLK = 128
PAIRS = 8
NNZ = 64
LIVE = 320
ITERS = 3
GROUPS = 4
GRAM = E // (C * X)

conf_rate = 0.5
ridge_weight = 0.5

bf16 = jnp.bfloat16
f32 = jnp.float32


def dot(a, b):
    return lax.dot_general(a, b, (((1,), (0,)), ((), ())), preferred_element_type=f32)


def split(a):
    hi = a.astype(bf16)
    return hi, (a - hi.astype(f32)).astype(bf16)


def offsets(live_ref, base):
    out = [0]
    for p in range(PAIRS - 1):
        out.append(out[-1] + live_ref[base + p])
    return out


USER_AT = GRAM
COUNT_AT = USER_AT + PAIRS
ITEM_AT = COUNT_AT + PAIRS
BLOCK_AT = ITEM_AT + GROUPS * PAIRS
LIVE_AT = BLOCK_AT + GROUPS
PACK = LIVE_AT + GROUPS


def pack_kernel(gram_ref, block_ref, live_ref, user_ref, item_ref, count_ref, out_ref):
    out_ref[...] = jnp.zeros(out_ref.shape, f32)
    items = item_ref[...].reshape(GROUPS * PAIRS, NNZ).astype(f32)
    for d in range(C * X):
        out_ref[d, :GRAM, :] = gram_ref[d * GRAM : (d + 1) * GRAM, :]
        out_ref[d, USER_AT : USER_AT + PAIRS, :NNZ] = user_ref[d % X].astype(f32)
        out_ref[d, COUNT_AT : COUNT_AT + PAIRS, :NNZ] = count_ref[d % X].astype(f32)
        out_ref[d, ITEM_AT : ITEM_AT + GROUPS * PAIRS, :NNZ] = items
        out_ref[d, BLOCK_AT : BLOCK_AT + GROUPS, :PAIRS] = block_ref[...].astype(f32)
        out_ref[d, LIVE_AT : LIVE_AT + GROUPS, :PAIRS] = live_ref[...].astype(f32)


def unpack_kernel(core_ref, part_ref, pack_ref, after_ref, gram_ref, own_ref, live_ref):
    gram = pack_ref[0, :GRAM, :]
    for d in range(1, C * X):
        gram = gram + pack_ref[d, :GRAM, :]
    gram_ref[...] = jnp.broadcast_to(gram[None], gram_ref.shape)
    for c in range(C):
        own_ref[c] = pack_ref[c * X + part_ref[0], BLOCK_AT:PACK, :].astype(jnp.int32)
    for s in range(X):
        row = pack_ref[core_ref[0] * X + s, pl.ds(LIVE_AT + part_ref[0], 1), :]
        live_ref[s : s + 1, :] = row.astype(jnp.int32)


def weight_kernel(core_ref, live_ref, pack_ref, out_ref, rows_ref):
    packs = [pack_ref[core_ref[0] * X + s] for s in range(X)]
    users = [pack[USER_AT : USER_AT + PAIRS] for pack in packs]
    counts = [pack[COUNT_AT : COUNT_AT + PAIRS] for pack in packs]
    table = jnp.concatenate(users + counts, axis=0).T[:NNZ]
    lane = lax.broadcasted_iota(jnp.int32, (NNZ, BLK), 1).astype(f32)
    slot = lax.broadcasted_iota(jnp.int32, (NNZ, BLK), 0)
    for s in range(X):
        offs = offsets(live_ref, s * PAIRS)
        for p in range(PAIRS):
            q = s * PAIRS + p
            hit = (table[:, q : q + 1] == lane) & (slot < live_ref[q])
            rows = jnp.where(hit, table[:, X * PAIRS + q : X * PAIRS + q + 1], 0.0)
            rows_ref[s, pl.ds(offs[p], NNZ), :] = rows
        out_ref[s * LIVE : (s + 1) * LIVE, :] = rows_ref[s, :LIVE, :].astype(bf16)


def place_kernel(part_ref, seen_ref, live_ref, pack_ref, out_ref, rows_ref):
    items = [
        pack_ref[c * X + part_ref[0], ITEM_AT : ITEM_AT + GROUPS * PAIRS, :] for c in range(C)
    ]
    table = jnp.concatenate(items, axis=0).T[:NNZ].astype(jnp.int32)
    lane = lax.broadcasted_iota(jnp.int32, (LIVE, BLK), 1)
    slot = lax.broadcasted_iota(jnp.int32, (NNZ, 1), 0)
    merged = jnp.full((LIVE, BLK), -1, jnp.int32)
    for d in range(C * GROUPS):
        offs = offsets(live_ref, d * PAIRS)
        for p in range(PAIRS):
            q = d * PAIRS + p
            spot = jnp.where(slot < seen_ref[q], table[:, q : q + 1] + p * BLK, -1)
            rows_ref[d, pl.ds(offs[p], NNZ), :] = jnp.broadcast_to(spot, (NNZ, BLK))
        merged = jnp.where(lane == d, rows_ref[d, :LIVE, :], merged)
    out_ref[...] = merged


def collect_kernel(turn_ref, block_ref, *refs):
    piece_refs, out_ref = refs[:-1], refs[-1]
    turns = [t for t in range(Y) if t != Y // 2]
    for q in range(C * GROUPS * PAIRS):
        turn, spot = turn_ref[q], block_ref[q]
        block = piece_refs[0][spot]
        for t, piece_ref in zip(turns[1:], piece_refs[1:]):
            block = jnp.where(turn == t, piece_ref[spot], block)
        out_ref[q] = block


def select_kernel(turn_ref, block_ref, place_ref, gram_ref, held_ref, last_ref, out_ref):
    gram = gram_ref[0]
    for d in range(1, Y):
        gram = gram + gram_ref[d]
    gram_hi, gram_lo = split(gram)
    lane = lax.broadcasted_iota(jnp.int32, (LIVE, PAIRS * BLK), 1)
    for d in range(C * GROUPS):
        blocks = []
        for p in range(PAIRS):
            q = d * PAIRS + p
            blocks.append(
                jnp.where(turn_ref[q] == Y // 2, last_ref[block_ref[q]], held_ref[q])
            )
        onehot = jnp.where(place_ref[:, d : d + 1] == lane, 1.0, 0.0).astype(bf16)
        rows = dot(onehot, jnp.concatenate(blocks, axis=0))
        out_ref[d, :LIVE, :] = rows.astype(bf16)
        out_ref[d, LIVE : LIVE + GRAM, :] = gram_hi
        out_ref[d, LIVE + GRAM :, :] = gram_lo


def solve_kernel(recv_ref, weight_ref, start_ref, out_ref):
    items = (recv_ref[:X, :LIVE, :] + recv_ref[X:, :LIVE, :]).reshape(X * LIVE, E)
    items_t = items.T
    weight = weight_ref[...]
    conf = weight.astype(f32) * conf_rate
    full = jnp.where(weight > 0, 1.0 + conf, 0.0).astype(bf16)
    gram = recv_ref[:, LIVE : LIVE + GRAM, :].astype(f32) + recv_ref[:, LIVE + GRAM :, :].astype(f32)
    gram = gram.reshape(E, E)
    eye = lax.broadcasted_iota(jnp.int32, (E, E), 0) == lax.broadcasted_iota(jnp.int32, (E, E), 1)
    base_hi, base_lo = split(
        gram * (E / (X * Z * Y * C * BLK)) + jnp.where(eye, ridge_weight, 0.0)
    )

    def operator(vectors):
        hi, lo = split(vectors)
        both = jnp.concatenate([hi, lo], axis=1)
        table = dot(items, both)
        table = conf * (table[:, :BLK] + table[:, BLK:])
        table_hi, table_lo = split(table)
        summed = dot(items_t, jnp.concatenate([table_hi, table_lo], axis=1))
        dense = dot(base_hi, both)
        return (
            (summed[:, :BLK] + summed[:, BLK:])
            + (dense[:, :BLK] + dense[:, BLK:])
            + dot(base_lo, hi)
        )

    x = start_ref[...].T
    remain = dot(items_t, full) - operator(x)
    direction = remain
    norm_now = jnp.sum(remain * remain, axis=0, keepdims=True)
    for turn in range(ITERS):
        image = operator(direction)
        step = norm_now / jnp.sum(direction * image, axis=0, keepdims=True)
        x = x + step * direction
        if turn < ITERS - 1:
            remain = remain - step * image
            norm_next = jnp.sum(remain * remain, axis=0, keepdims=True)
            direction = remain + norm_next / norm_now * direction
            norm_now = norm_next
    out_ref[...] = x.T


def vmem():
    return pl.BlockSpec(memory_space=pltpu.VMEM)


def smem():
    return pl.BlockSpec(memory_space=pltpu.SMEM)


def spread(value, axis, size):
    return lax.all_to_all(jnp.broadcast_to(value[None], (size,) + value.shape), axis, 0, 0, tiled=True)


def from_next(value):
    return lax.ppermute(value, "y", [(i, (i - 1) % Y) for i in range(Y)])


def from_last(value):
    return lax.ppermute(value, "y", [(i, (i + 1) % Y) for i in range(Y)])


def call(kernel, out, ins, scratch=(), flops=1_000_000, nbytes=400_000):
    return pl.pallas_call(
        kernel,
        out_shape=out,
        in_specs=ins,
        out_specs=[vmem() for _ in out] if isinstance(out, tuple) else vmem(),
        scratch_shapes=list(scratch),
        compiler_params=pltpu.CompilerParams(vmem_limit_bytes=24 * 1024 * 1024),
        cost_estimate=pl.CostEstimate(flops=flops, bytes_accessed=nbytes, transcendentals=0),
    )


def local(block_ids, pair_live, user_rows, item_rows, counts, item_emb, user_emb):
    core = lax.axis_index("core")
    part = lax.axis_index("x")
    own_block = item_emb[0].astype(bf16)
    with jax.named_scope("gather_z"):
        column = lax.all_gather(own_block, "z", axis=0, tiled=True)
    with jax.named_scope("gather_y"):
        ups, downs = [column], [column]
        for _ in range(Y // 2 - 1):
            ups.append(from_next(ups[-1]))
            downs.append(from_last(downs[-1]))
        ups.append(from_next(ups[-1]))
        pieces = [piece.reshape(Z, BLK, E) for piece in ups + downs[:0:-1]]

    with jax.named_scope("gramian"):
        gram = lax.dot_general(
            column, column, (((0,), (0,)), ((), ())), preferred_element_type=f32
        )
    with jax.named_scope("small_exchange"):
        pack = call(
            pack_kernel, jax.ShapeDtypeStruct((C * X, PACK, BLK), f32), [vmem()] * 6
        )(
            gram,
            block_ids[:, 0],
            pair_live[:, 0],
            user_rows[:, 0],
            item_rows[:, 0],
            counts[:, 0],
        )
        pack = lax.all_to_all(pack, ("core", "x"), 0, 0, tiled=True)
        gram, own, user_live = call(
            unpack_kernel,
            (
                jax.ShapeDtypeStruct((Y, GRAM, E), f32),
                jax.ShapeDtypeStruct((C, PACK - BLOCK_AT, BLK), jnp.int32),
                jax.ShapeDtypeStruct((X, BLK), jnp.int32),
            ),
            [smem()] * 2 + [vmem(), pl.BlockSpec(memory_space=pl.ANY)],
        )(core.reshape(1), part.reshape(1), pack, downs[-2])
    with jax.named_scope("gramian"):
        gram = lax.all_to_all(gram, "y", 0, 0, tiled=True)

    with jax.named_scope("indices"):
        own, user_live = own[:, :, :PAIRS], user_live[:, :PAIRS].reshape(-1)
        ids, live = own[:, :GROUPS].reshape(-1), own[:, GROUPS:].reshape(-1)
        z_of, y_of, c_of = ids // (Y * C), ids // C % Y, ids % C
        turns = (y_of - lax.axis_index("y")) % Y
        spots = jnp.clip(z_of, 0, Z - 1)
        seen = jnp.where(c_of == core, live, 0)

    with jax.named_scope("place"):
        place = call(
            place_kernel,
            jax.ShapeDtypeStruct((LIVE, BLK), jnp.int32),
            [smem()] * 3 + [vmem()],
            [pltpu.VMEM((C * GROUPS, LIVE + NNZ, BLK), jnp.int32)],
        )(part.reshape(1), seen, live, pack)
    with jax.named_scope("weights"):
        weight = call(
            weight_kernel,
            jax.ShapeDtypeStruct((X * LIVE, BLK), bf16),
            [smem()] * 2 + [vmem()],
            [pltpu.VMEM((X, LIVE + NNZ, BLK), f32)],
        )(core.reshape(1), user_live, pack)
    with jax.named_scope("collect"):
        last = pieces.pop(Y // 2)
        held = call(
            collect_kernel,
            jax.ShapeDtypeStruct((C * GROUPS * PAIRS, BLK, E), bf16),
            [smem()] * 2 + [vmem()] * len(pieces),
            nbytes=4_000_000,
        )(turns, spots, *pieces)
    with jax.named_scope("select"):
        chosen = call(
            select_kernel,
            jax.ShapeDtypeStruct((C * GROUPS, LIVE + 2 * GRAM, E), bf16),
            [smem()] * 2 + [vmem()] * 4,
            flops=700_000_000,
            nbytes=4_000_000,
        )(turns, spots, place, gram, held, last)
    with jax.named_scope("exchange"):
        received = lax.all_to_all(chosen, ("core", "x"), 0, 0, tiled=True)
    with jax.named_scope("solve"):
        start = lax.dynamic_slice_in_dim(user_emb, part * BLK, BLK, 0)
        solved = call(
            solve_kernel,
            jax.ShapeDtypeStruct((BLK, E), f32),
            [vmem()] * 3,
            flops=800_000_000,
            nbytes=1_200_000,
        )(received, weight, start)
    with jax.named_scope("gather_x"):
        return spread(solved, "x", X).reshape(X * BLK, E)


def solution(mesh):
    grid = Mesh(mesh.devices.reshape(Z, Y, C, X), ("z", "y", "core", "x"))
    users = ("z", "y", "core")
    return jax.shard_map(
        local,
        mesh=grid,
        in_specs=(
            P(users, "x", None),
            P(users, "x", None),
            P(users, "x", None, None),
            P(users, "x", None, None),
            P(users, "x", None, None),
            P("x", users, None),
            P(users, None),
        ),
        out_specs=P(users, None),
        check_vma=False,
    )
```

```python
import functools

import jax
import jax.numpy as jnp
from jax import lax
from jax.experimental import pallas as pl
from jax.experimental.pallas import tpu as pltpu
from jax.sharding import Mesh, PartitionSpec as P

Z, Y, C, X = 12, 8, 2, 4
E = 128
BLK = 128
PAIRS = 8
NNZ = 64
LIVE = 320
ITERS = 3
GROUPS = 4
HALF = E // 2
GRAM = HALF + HALF // 2

conf_rate = 0.5
ridge_weight = 0.5

bf16 = jnp.bfloat16
f32 = jnp.float32


def dot(a, b):
    return lax.dot_general(a, b, (((1,), (0,)), ((), ())), preferred_element_type=f32)


def split(a):
    hi = a.astype(bf16)
    return hi, (a - hi.astype(f32)).astype(bf16)


def offsets(live_ref, base):
    out = [0]
    for p in range(PAIRS - 1):
        out.append(out[-1] + live_ref[base + p])
    return out


COUNT_AT = PAIRS
ITEM_AT = COUNT_AT + PAIRS
BLOCK_AT = ITEM_AT + GROUPS * PAIRS
LIVE_AT = BLOCK_AT + GROUPS
PACK = LIVE_AT + GROUPS


def fetch(pairs, sems):
    copies = [pltpu.make_async_copy(src, dst, sems.at[i]) for i, (src, dst) in enumerate(pairs)]
    for copy in copies:
        copy.start()
    for copy in copies:
        copy.wait()


def square(rows):
    return lax.dot_general(rows, rows, (((0,), (0,)), ((), ())), preferred_element_type=f32)


def pack_kernel(block_hbm, live_hbm, user_hbm, item_hbm, count_hbm, out_ref, *scratch):
    block_ref, live_ref, user_ref, item_ref, count_ref, sems = scratch
    sources = (block_hbm, live_hbm, user_hbm, item_hbm, count_hbm)
    fetch(list(zip(sources, scratch[:-1])), sems)
    out_ref[...] = jnp.zeros(out_ref.shape, f32)
    items = item_ref[...].reshape(GROUPS * PAIRS, NNZ).astype(f32)
    for d in range(C * X):
        out_ref[d, :PAIRS, :NNZ] = user_ref[d % X].astype(f32)
        out_ref[d, COUNT_AT : COUNT_AT + PAIRS, :NNZ] = count_ref[d % X].astype(f32)
        out_ref[d, ITEM_AT : ITEM_AT + GROUPS * PAIRS, :NNZ] = items
        out_ref[d, BLOCK_AT : BLOCK_AT + GROUPS, :PAIRS] = block_ref[...].astype(f32)
        out_ref[d, LIVE_AT : LIVE_AT + GROUPS, :PAIRS] = live_ref[...].astype(f32)


def unpack_kernel(core_ref, part_ref, pack_ref, after_ref, own_ref, live_ref):
    for c in range(C):
        own_ref[c] = pack_ref[c * X + part_ref[0], BLOCK_AT:PACK, :].astype(jnp.int32)
    for s in range(X):
        row = pack_ref[core_ref[0] * X + s, pl.ds(LIVE_AT + part_ref[0], 1), :]
        live_ref[s : s + 1, :] = row.astype(jnp.int32)


def weight_kernel(core_ref, live_ref, pack_ref, out_ref, rows_ref):
    packs = [pack_ref[core_ref[0] * X + s] for s in range(X)]
    users = [pack[:PAIRS] for pack in packs]
    counts = [pack[COUNT_AT : COUNT_AT + PAIRS] for pack in packs]
    table = jnp.concatenate(users + counts, axis=0).T[:NNZ]
    lane = lax.broadcasted_iota(jnp.int32, (NNZ, BLK), 1).astype(f32)
    slot = lax.broadcasted_iota(jnp.int32, (NNZ, BLK), 0)
    for s in range(X):
        offs = offsets(live_ref, s * PAIRS)
        for p in range(PAIRS):
            q = s * PAIRS + p
            hit = (table[:, q : q + 1] == lane) & (slot < live_ref[q])
            rows = jnp.where(hit, table[:, X * PAIRS + q : X * PAIRS + q + 1], 0.0)
            rows_ref[s, pl.ds(offs[p], NNZ), :] = rows
        out_ref[s * LIVE : (s + 1) * LIVE, :] = rows_ref[s, :LIVE, :].astype(bf16)


def place_kernel(part_ref, seen_ref, live_ref, pack_ref, out_ref, rows_ref):
    items = [
        pack_ref[c * X + part_ref[0], ITEM_AT : ITEM_AT + GROUPS * PAIRS, :] for c in range(C)
    ]
    table = jnp.concatenate(items, axis=0).T[:NNZ].astype(jnp.int32)
    lane = lax.broadcasted_iota(jnp.int32, (LIVE, BLK), 1)
    slot = lax.broadcasted_iota(jnp.int32, (NNZ, 1), 0)
    merged = jnp.full((LIVE, BLK), -1, jnp.int32)
    for d in range(C * GROUPS):
        offs = offsets(live_ref, d * PAIRS)
        for p in range(PAIRS):
            q = d * PAIRS + p
            spot = jnp.where(slot < seen_ref[q], table[:, q : q + 1] + p * BLK, -1)
            rows_ref[d, pl.ds(offs[p], NNZ), :] = jnp.broadcast_to(spot, (NNZ, BLK))
        merged = jnp.where(lane == d, rows_ref[d, :LIVE, :], merged)
    out_ref[...] = merged


def collect_kernel(turn_ref, block_ref, *refs):
    piece_refs, (out_ref, gram_ref, held, sems) = refs[:-4], refs[-4:]
    fetch([(piece_ref, held.at[i]) for i, piece_ref in enumerate(piece_refs)], sems)
    for q in range(C * GROUPS * PAIRS):
        turn = turn_ref[q]
        place = jnp.minimum(jnp.where(turn > Y // 2, turn - 1, turn), Y - 2)
        out_ref[q] = held[place, block_ref[q]]
    gram = square(held[0].reshape(Z * BLK, E))
    for i in range(1, Y - 1):
        gram = gram + square(held[i].reshape(Z * BLK, E))
    gram_ref[...] = gram


def select_kernel(
    turn_ref, block_ref, place_ref, gram_ref, held_ref, last_hbm, out_ref, last_ref, sems
):
    fetch([(last_hbm, last_ref)], sems)
    gram = gram_ref[...] + square(last_ref[...].reshape(Z * BLK, E))
    corner = gram[:HALF, HALF:]
    gram = jnp.concatenate(
        [
            jnp.concatenate([gram[:HALF, :HALF], gram[HALF:, HALF:]], axis=1),
            jnp.concatenate([corner[: HALF // 2], corner[HALF // 2 :]], axis=1),
        ],
        axis=0,
    )
    gram_hi, gram_lo = split(gram)
    lane = lax.broadcasted_iota(jnp.int32, (LIVE, PAIRS * BLK), 1)
    for d in range(C * GROUPS):
        blocks = []
        for p in range(PAIRS):
            q = d * PAIRS + p
            blocks.append(
                jnp.where(turn_ref[q] == Y // 2, last_ref[block_ref[q]], held_ref[q])
            )
        onehot = jnp.where(place_ref[:, d : d + 1] == lane, 1.0, 0.0).astype(bf16)
        rows = dot(onehot, jnp.concatenate(blocks, axis=0))
        out_ref[d, :LIVE, :] = rows.astype(bf16)
        out_ref[d, LIVE : LIVE + GRAM, :] = gram_hi
        out_ref[d, LIVE + GRAM :, :] = gram_lo


def solve_kernel(recv_ref, weight_ref, start_ref, out_ref):
    items = (recv_ref[:X, :LIVE, :] + recv_ref[X:, :LIVE, :]).reshape(X * LIVE, E)
    items_t = items.T
    weight = weight_ref[...]
    conf = weight.astype(f32) * conf_rate
    full = jnp.where(weight > 0, 1.0 + conf, 0.0).astype(bf16)
    gram = recv_ref[:, LIVE : LIVE + GRAM, :].astype(f32) + recv_ref[:, LIVE + GRAM :, :].astype(f32)
    gram = jnp.sum(gram, axis=0)
    corner = jnp.concatenate([gram[HALF:, :HALF], gram[HALF:, HALF:]], axis=0)
    gram = jnp.concatenate(
        [
            jnp.concatenate([gram[:HALF, :HALF], corner], axis=1),
            jnp.concatenate([corner.T, gram[:HALF, HALF:]], axis=1),
        ],
        axis=0,
    )
    eye = lax.broadcasted_iota(jnp.int32, (E, E), 0) == lax.broadcasted_iota(jnp.int32, (E, E), 1)
    base_hi, base_lo = split(
        gram * (E / (X * Z * Y * C * BLK)) + jnp.where(eye, ridge_weight, 0.0)
    )

    def operator(vectors):
        hi, lo = split(vectors)
        both = jnp.concatenate([hi, lo], axis=1)
        table = dot(items, both)
        table = conf * (table[:, :BLK] + table[:, BLK:])
        table_hi, table_lo = split(table)
        summed = dot(items_t, jnp.concatenate([table_hi, table_lo], axis=1))
        dense = dot(base_hi, both)
        return (
            (summed[:, :BLK] + summed[:, BLK:])
            + (dense[:, :BLK] + dense[:, BLK:])
            + dot(base_lo, hi)
        )

    x = start_ref[...].T
    remain = dot(items_t, full) - operator(x)
    direction = remain
    norm_now = jnp.sum(remain * remain, axis=0, keepdims=True)
    for turn in range(ITERS):
        image = operator(direction)
        step = norm_now / jnp.sum(direction * image, axis=0, keepdims=True)
        x = x + step * direction
        if turn < ITERS - 1:
            remain = remain - step * image
            norm_next = jnp.sum(remain * remain, axis=0, keepdims=True)
            direction = remain + norm_next / norm_now * direction
            norm_now = norm_next
    out_ref[...] = x.T


def vmem():
    return pl.BlockSpec(memory_space=pltpu.VMEM)


def smem():
    return pl.BlockSpec(memory_space=pltpu.SMEM)


def hbm():
    return pl.BlockSpec(memory_space=pl.ANY)


def spread(value, axis, size):
    return lax.all_to_all(jnp.broadcast_to(value[None], (size,) + value.shape), axis, 0, 0, tiled=True)


def from_next(value):
    return lax.ppermute(value, "y", [(i, (i - 1) % Y) for i in range(Y)])


def from_last(value):
    return lax.ppermute(value, "y", [(i, (i + 1) % Y) for i in range(Y)])


def call(kernel, out, ins, scratch=(), flops=1_000_000, nbytes=400_000):
    return pl.pallas_call(
        kernel,
        out_shape=out,
        in_specs=ins,
        out_specs=[vmem() for _ in out] if isinstance(out, tuple) else vmem(),
        scratch_shapes=list(scratch),
        compiler_params=pltpu.CompilerParams(vmem_limit_bytes=24 * 1024 * 1024),
        cost_estimate=pl.CostEstimate(flops=flops, bytes_accessed=nbytes, transcendentals=0),
    )


def local(block_ids, pair_live, user_rows, item_rows, counts, item_emb, user_emb):
    core = lax.axis_index("core")
    part = lax.axis_index("x")
    own_block = item_emb[0].astype(bf16)
    with jax.named_scope("gather_z"):
        column = lax.all_gather(own_block, "z", axis=0, tiled=True)
    with jax.named_scope("gather_y"):
        ups, downs = [column], [column]
        for _ in range(Y // 2 - 1):
            ups.append(from_next(ups[-1]))
            downs.append(from_last(downs[-1]))
        ups.append(from_next(ups[-1]))
        pieces = [piece.reshape(Z, BLK, E) for piece in ups + downs[:0:-1]]

    with jax.named_scope("small_exchange"):
        ints = (
            block_ids[:, 0],
            pair_live[:, 0],
            user_rows[:, 0],
            item_rows[:, 0],
            counts[:, 0],
        )
        pack = call(
            pack_kernel,
            jax.ShapeDtypeStruct((C * X, PACK, BLK), f32),
            [hbm()] * len(ints),
            [pltpu.VMEM(value.shape, value.dtype) for value in ints]
            + [pltpu.SemaphoreType.DMA((len(ints),))],
        )(*ints)
        pack = lax.all_to_all(pack, ("core", "x"), 0, 0, tiled=True)
        own, user_live = call(
            unpack_kernel,
            (
                jax.ShapeDtypeStruct((C, PACK - BLOCK_AT, BLK), jnp.int32),
                jax.ShapeDtypeStruct((X, BLK), jnp.int32),
            ),
            [smem()] * 2 + [vmem(), hbm()],
        )(core.reshape(1), part.reshape(1), pack, ups[-2])

    with jax.named_scope("indices"):
        own, user_live = own[:, :, :PAIRS], user_live[:, :PAIRS].reshape(-1)
        ids, live = own[:, :GROUPS].reshape(-1), own[:, GROUPS:].reshape(-1)
        z_of, y_of, c_of = ids // (Y * C), ids // C % Y, ids % C
        turns = (y_of - lax.axis_index("y")) % Y
        spots = jnp.clip(z_of, 0, Z - 1)
        seen = jnp.where(c_of == core, live, 0)

    with jax.named_scope("place"):
        place = call(
            place_kernel,
            jax.ShapeDtypeStruct((LIVE, BLK), jnp.int32),
            [smem()] * 3 + [vmem()],
            [pltpu.VMEM((C * GROUPS, LIVE + NNZ, BLK), jnp.int32)],
        )(part.reshape(1), seen, live, pack)
    with jax.named_scope("weights"):
        weight = call(
            weight_kernel,
            jax.ShapeDtypeStruct((X * LIVE, BLK), bf16),
            [smem()] * 2 + [vmem()],
            [pltpu.VMEM((X, LIVE + NNZ, BLK), f32)],
        )(core.reshape(1), user_live, pack)
    with jax.named_scope("collect"):
        last = pieces.pop(Y // 2)
        held, gram = call(
            collect_kernel,
            (
                jax.ShapeDtypeStruct((C * GROUPS * PAIRS, BLK, E), bf16),
                jax.ShapeDtypeStruct((E, E), f32),
            ),
            [smem()] * 2 + [hbm()] * len(pieces),
            [
                pltpu.VMEM((Y - 1, Z, BLK, E), bf16),
                pltpu.SemaphoreType.DMA((Y - 1,)),
            ],
            nbytes=4_000_000,
        )(turns, spots, *pieces)
    with jax.named_scope("select"):
        chosen = call(
            select_kernel,
            jax.ShapeDtypeStruct((C * GROUPS, LIVE + 2 * GRAM, E), bf16),
            [smem()] * 2 + [vmem()] * 3 + [hbm()],
            [pltpu.VMEM((Z, BLK, E), bf16), pltpu.SemaphoreType.DMA((1,))],
            flops=700_000_000,
            nbytes=4_000_000,
        )(turns, spots, place, gram, held, last)
    with jax.named_scope("exchange"):
        received = lax.all_to_all(chosen, ("core", "x"), 0, 0, tiled=True)
    with jax.named_scope("solve"):
        start = lax.dynamic_slice_in_dim(user_emb, part * BLK, BLK, 0)
        solved = call(
            solve_kernel,
            jax.ShapeDtypeStruct((BLK, E), f32),
            [vmem()] * 3,
            flops=800_000_000,
            nbytes=1_200_000,
        )(received, weight, start)
    with jax.named_scope("gather_x"):
        return spread(solved, "x", X).reshape(X * BLK, E)


def solution(mesh):
    grid = Mesh(mesh.devices.reshape(Z, Y, C, X), ("z", "y", "core", "x"))
    users = ("z", "y", "core")
    return jax.shard_map(
        local,
        mesh=grid,
        in_specs=(
            P(users, "x", None),
            P(users, "x", None),
            P(users, "x", None, None),
            P(users, "x", None, None),
            P(users, "x", None, None),
            P("x", users, None),
            P(users, None),
        ),
        out_specs=P(users, None),
        check_vma=False,
    )
```

```python
import functools

import jax
import jax.numpy as jnp
from jax import lax
from jax.experimental import pallas as pl
from jax.experimental.pallas import tpu as pltpu
from jax.sharding import Mesh, PartitionSpec as P

Z, Y, C, X = 12, 8, 2, 4
E = 128
BLK = 128
PAIRS = 8
NNZ = 64
LIVE = 320
ITERS = 3
GROUPS = 4
HALF = E // 2
GRAM = HALF + HALF // 2

conf_rate = 0.5
ridge_weight = 0.5

bf16 = jnp.bfloat16
f32 = jnp.float32


def dot(a, b):
    return lax.dot_general(a, b, (((1,), (0,)), ((), ())), preferred_element_type=f32)


def split(a):
    hi = a.astype(bf16)
    return hi, (a - hi.astype(f32)).astype(bf16)


def offsets(live_ref, base):
    out = [0]
    for p in range(PAIRS - 1):
        out.append(out[-1] + live_ref[base + p])
    return out


COUNT_AT = PAIRS
ITEM_AT = COUNT_AT + PAIRS
BLOCK_AT = ITEM_AT + GROUPS * PAIRS
LIVE_AT = BLOCK_AT + GROUPS
PACK = LIVE_AT + GROUPS


def fetch(pairs, sems):
    copies = [pltpu.make_async_copy(src, dst, sems.at[i]) for i, (src, dst) in enumerate(pairs)]
    for copy in copies:
        copy.start()
    for copy in copies:
        copy.wait()


def square(rows):
    return lax.dot_general(rows, rows, (((0,), (0,)), ((), ())), preferred_element_type=f32)


def pack_kernel(slots_ref, blocks_ref, out_ref):
    out_ref[...] = jnp.zeros(out_ref.shape, f32)
    items = slots_ref[:, 2 * PAIRS :, :].reshape(GROUPS * PAIRS, NNZ)
    for d in range(C * X):
        out_ref[d, : 2 * PAIRS, :NNZ] = slots_ref[d % X, : 2 * PAIRS, :]
        out_ref[d, ITEM_AT : ITEM_AT + GROUPS * PAIRS, :NNZ] = items
        out_ref[d, BLOCK_AT:, :PAIRS] = blocks_ref[...]


def unpack_kernel(core_ref, part_ref, pack_ref, after_ref, own_ref, live_ref):
    for c in range(C):
        own_ref[c] = pack_ref[c * X + part_ref[0], BLOCK_AT:PACK, :].astype(jnp.int32)
    for s in range(X):
        row = pack_ref[core_ref[0] * X + s, pl.ds(LIVE_AT + part_ref[0], 1), :]
        live_ref[s : s + 1, :] = row.astype(jnp.int32)


def weight_kernel(core_ref, live_ref, pack_ref, out_ref, rows_ref):
    packs = [pack_ref[core_ref[0] * X + s] for s in range(X)]
    users = [pack[:PAIRS] for pack in packs]
    counts = [pack[COUNT_AT : COUNT_AT + PAIRS] for pack in packs]
    table = jnp.concatenate(users + counts, axis=0).T[:NNZ]
    lane = lax.broadcasted_iota(jnp.int32, (NNZ, BLK), 1).astype(f32)
    slot = lax.broadcasted_iota(jnp.int32, (NNZ, BLK), 0)
    for s in range(X):
        offs = offsets(live_ref, s * PAIRS)
        for p in range(PAIRS):
            q = s * PAIRS + p
            hit = (table[:, q : q + 1] == lane) & (slot < live_ref[q])
            rows = jnp.where(hit, table[:, X * PAIRS + q : X * PAIRS + q + 1], 0.0)
            rows_ref[s, pl.ds(offs[p], NNZ), :] = rows
        out_ref[s * LIVE : (s + 1) * LIVE, :] = rows_ref[s, :LIVE, :].astype(bf16)


def place_kernel(part_ref, seen_ref, live_ref, pack_ref, out_ref, rows_ref):
    items = [
        pack_ref[c * X + part_ref[0], ITEM_AT : ITEM_AT + GROUPS * PAIRS, :] for c in range(C)
    ]
    table = jnp.concatenate(items, axis=0).T[:NNZ].astype(jnp.int32)
    lane = lax.broadcasted_iota(jnp.int32, (LIVE, BLK), 1)
    slot = lax.broadcasted_iota(jnp.int32, (NNZ, 1), 0)
    merged = jnp.full((LIVE, BLK), -1, jnp.int32)
    for d in range(C * GROUPS):
        offs = offsets(live_ref, d * PAIRS)
        for p in range(PAIRS):
            q = d * PAIRS + p
            spot = jnp.where(slot < seen_ref[q], table[:, q : q + 1] + p * BLK, -1)
            rows_ref[d, pl.ds(offs[p], NNZ), :] = jnp.broadcast_to(spot, (NNZ, BLK))
        merged = jnp.where(lane == d, rows_ref[d, :LIVE, :], merged)
    out_ref[...] = merged


def collect_kernel(turn_ref, block_ref, *refs):
    piece_refs, (out_ref, gram_ref, held, sems) = refs[:-4], refs[-4:]
    fetch([(piece_ref, held.at[i]) for i, piece_ref in enumerate(piece_refs)], sems)
    for q in range(C * GROUPS * PAIRS):
        turn = turn_ref[q]
        place = jnp.minimum(jnp.where(turn > Y // 2, turn - 1, turn), Y - 2)
        out_ref[q] = held[place, block_ref[q]]
    gram = square(held[0].reshape(Z * BLK, E))
    for i in range(1, Y - 1):
        gram = gram + square(held[i].reshape(Z * BLK, E))
    gram_ref[...] = gram


def select_kernel(
    turn_ref, block_ref, place_ref, gram_ref, held_ref, last_hbm, out_ref, last_ref, sems
):
    fetch([(last_hbm, last_ref)], sems)
    gram = gram_ref[...] + square(last_ref[...].reshape(Z * BLK, E))
    corner = gram[:HALF, HALF:]
    gram = jnp.concatenate(
        [
            jnp.concatenate([gram[:HALF, :HALF], gram[HALF:, HALF:]], axis=1),
            jnp.concatenate([corner[: HALF // 2], corner[HALF // 2 :]], axis=1),
        ],
        axis=0,
    )
    gram_hi, gram_lo = split(gram)
    lane = lax.broadcasted_iota(jnp.int32, (LIVE, PAIRS * BLK), 1)
    for d in range(C * GROUPS):
        blocks = []
        for p in range(PAIRS):
            q = d * PAIRS + p
            blocks.append(
                jnp.where(turn_ref[q] == Y // 2, last_ref[block_ref[q]], held_ref[q])
            )
        onehot = jnp.where(place_ref[:, d : d + 1] == lane, 1.0, 0.0).astype(bf16)
        rows = dot(onehot, jnp.concatenate(blocks, axis=0))
        out_ref[d, :LIVE, :] = rows.astype(bf16)
        out_ref[d, LIVE : LIVE + GRAM, :] = gram_hi
        out_ref[d, LIVE + GRAM :, :] = gram_lo


def solve_kernel(recv_ref, weight_ref, start_ref, out_ref):
    items = (recv_ref[:X, :LIVE, :] + recv_ref[X:, :LIVE, :]).reshape(X * LIVE, E)
    items_t = items.T
    weight = weight_ref[...]
    conf = weight.astype(f32) * conf_rate
    full = jnp.where(weight > 0, 1.0 + conf, 0.0).astype(bf16)
    gram = recv_ref[:, LIVE : LIVE + GRAM, :].astype(f32) + recv_ref[:, LIVE + GRAM :, :].astype(f32)
    gram = jnp.sum(gram, axis=0)
    corner = jnp.concatenate([gram[HALF:, :HALF], gram[HALF:, HALF:]], axis=0)
    gram = jnp.concatenate(
        [
            jnp.concatenate([gram[:HALF, :HALF], corner], axis=1),
            jnp.concatenate([corner.T, gram[:HALF, HALF:]], axis=1),
        ],
        axis=0,
    )
    eye = lax.broadcasted_iota(jnp.int32, (E, E), 0) == lax.broadcasted_iota(jnp.int32, (E, E), 1)
    base_hi, base_lo = split(
        gram * (E / (X * Z * Y * C * BLK)) + jnp.where(eye, ridge_weight, 0.0)
    )

    def operator(vectors):
        hi, lo = split(vectors)
        both = jnp.concatenate([hi, lo], axis=1)
        table = dot(items, both)
        table = conf * (table[:, :BLK] + table[:, BLK:])
        table_hi, table_lo = split(table)
        summed = dot(items_t, jnp.concatenate([table_hi, table_lo], axis=1))
        dense = dot(base_hi, both)
        return (
            (summed[:, :BLK] + summed[:, BLK:])
            + (dense[:, :BLK] + dense[:, BLK:])
            + dot(base_lo, hi)
        )

    x = start_ref[...].T
    remain = dot(items_t, full) - operator(x)
    direction = remain
    norm_now = jnp.sum(remain * remain, axis=0, keepdims=True)
    for turn in range(ITERS):
        image = operator(direction)
        step = norm_now / jnp.sum(direction * image, axis=0, keepdims=True)
        x = x + step * direction
        if turn < ITERS - 1:
            remain = remain - step * image
            norm_next = jnp.sum(remain * remain, axis=0, keepdims=True)
            direction = remain + norm_next / norm_now * direction
            norm_now = norm_next
    out_ref[...] = x.T


def vmem():
    return pl.BlockSpec(memory_space=pltpu.VMEM)


def smem():
    return pl.BlockSpec(memory_space=pltpu.SMEM)


def hbm():
    return pl.BlockSpec(memory_space=pl.ANY)


def spread(value, axis, size):
    return lax.all_to_all(jnp.broadcast_to(value[None], (size,) + value.shape), axis, 0, 0, tiled=True)


def from_next(value):
    return lax.ppermute(value, "y", [(i, (i - 1) % Y) for i in range(Y)])


def from_last(value):
    return lax.ppermute(value, "y", [(i, (i + 1) % Y) for i in range(Y)])


def call(kernel, out, ins, scratch=(), flops=1_000_000, nbytes=400_000):
    return pl.pallas_call(
        kernel,
        out_shape=out,
        in_specs=ins,
        out_specs=[vmem() for _ in out] if isinstance(out, tuple) else vmem(),
        scratch_shapes=list(scratch),
        compiler_params=pltpu.CompilerParams(vmem_limit_bytes=24 * 1024 * 1024),
        cost_estimate=pl.CostEstimate(flops=flops, bytes_accessed=nbytes, transcendentals=0),
    )


def local(block_ids, pair_live, user_rows, item_rows, counts, item_emb, user_emb):
    core = lax.axis_index("core")
    part = lax.axis_index("x")
    own_block = item_emb[0].astype(bf16)
    with jax.named_scope("gather_z"):
        column = lax.all_gather(own_block, "z", axis=0, tiled=True)
    with jax.named_scope("gather_y"):
        ups, downs = [column], [column]
        for _ in range(Y // 2 - 1):
            ups.append(from_next(ups[-1]))
            downs.append(from_last(downs[-1]))
        downs.append(from_last(downs[-1]))
        pieces = [piece.reshape(Z, BLK, E) for piece in ups + downs[:0:-1]]

    with jax.named_scope("small_exchange"):
        slots = jnp.concatenate([user_rows[:, 0], counts[:, 0], item_rows[:, 0]], axis=1)
        blocks = jnp.concatenate([block_ids[:, 0], pair_live[:, 0]], axis=0)
        pack = call(
            pack_kernel, jax.ShapeDtypeStruct((C * X, PACK, BLK), f32), [vmem()] * 2
        )(slots.astype(f32), blocks.astype(f32))
        pack = lax.all_to_all(pack, ("core", "x"), 0, 0, tiled=True)
        own, user_live = call(
            unpack_kernel,
            (
                jax.ShapeDtypeStruct((C, PACK - BLOCK_AT, BLK), jnp.int32),
                jax.ShapeDtypeStruct((X, BLK), jnp.int32),
            ),
            [smem()] * 2 + [vmem(), hbm()],
        )(core.reshape(1), part.reshape(1), pack, downs[-2])

    with jax.named_scope("indices"):
        own, user_live = own[:, :, :PAIRS], user_live[:, :PAIRS].reshape(-1)
        ids, live = own[:, :GROUPS].reshape(-1), own[:, GROUPS:].reshape(-1)
        z_of, y_of, c_of = ids // (Y * C), ids // C % Y, ids % C
        turns = (y_of - lax.axis_index("y")) % Y
        spots = jnp.clip(z_of, 0, Z - 1)
        seen = jnp.where(c_of == core, live, 0)

    with jax.named_scope("place"):
        place = call(
            place_kernel,
            jax.ShapeDtypeStruct((LIVE, BLK), jnp.int32),
            [smem()] * 3 + [vmem()],
            [pltpu.VMEM((C * GROUPS, LIVE + NNZ, BLK), jnp.int32)],
        )(part.reshape(1), seen, live, pack)
    with jax.named_scope("weights"):
        weight = call(
            weight_kernel,
            jax.ShapeDtypeStruct((X * LIVE, BLK), bf16),
            [smem()] * 2 + [vmem()],
            [pltpu.VMEM((X, LIVE + NNZ, BLK), f32)],
        )(core.reshape(1), user_live, pack)
    with jax.named_scope("collect"):
        last = pieces.pop(Y // 2)
        held, gram = call(
            collect_kernel,
            (
                jax.ShapeDtypeStruct((C * GROUPS * PAIRS, BLK, E), bf16),
                jax.ShapeDtypeStruct((E, E), f32),
            ),
            [smem()] * 2 + [hbm()] * len(pieces),
            [
                pltpu.VMEM((Y - 1, Z, BLK, E), bf16),
                pltpu.SemaphoreType.DMA((Y - 1,)),
            ],
            nbytes=4_000_000,
        )(turns, spots, *pieces)
    with jax.named_scope("select"):
        chosen = call(
            select_kernel,
            jax.ShapeDtypeStruct((C * GROUPS, LIVE + 2 * GRAM, E), bf16),
            [smem()] * 2 + [vmem()] * 3 + [hbm()],
            [pltpu.VMEM((Z, BLK, E), bf16), pltpu.SemaphoreType.DMA((1,))],
            flops=700_000_000,
            nbytes=4_000_000,
        )(turns, spots, place, gram, held, last)
    with jax.named_scope("exchange"):
        received = lax.all_to_all(chosen, ("core", "x"), 0, 0, tiled=True)
    with jax.named_scope("solve"):
        start = lax.dynamic_slice_in_dim(user_emb, part * BLK, BLK, 0)
        solved = call(
            solve_kernel,
            jax.ShapeDtypeStruct((BLK, E), f32),
            [vmem()] * 3,
            flops=800_000_000,
            nbytes=1_200_000,
        )(received, weight, start)
    with jax.named_scope("gather_x"):
        return spread(solved, "x", X).reshape(X * BLK, E)


def solution(mesh):
    grid = Mesh(mesh.devices.reshape(Z, Y, C, X), ("z", "y", "core", "x"))
    users = ("z", "y", "core")
    return jax.shard_map(
        local,
        mesh=grid,
        in_specs=(
            P(users, "x", None),
            P(users, "x", None),
            P(users, "x", None, None),
            P(users, "x", None, None),
            P(users, "x", None, None),
            P("x", users, None),
            P(users, None),
        ),
        out_specs=P(users, None),
        check_vma=False,
    )
```

```python
import functools

import jax
import jax.numpy as jnp
from jax import lax
from jax.experimental import pallas as pl
from jax.experimental.pallas import tpu as pltpu
from jax.sharding import Mesh, PartitionSpec as P

Z, Y, C, X = 12, 8, 2, 4
E = 128
BLK = 128
PAIRS = 8
NNZ = 64
LIVE = 320
ITERS = 3
GROUPS = 4
HALF = E // 2
GRAM = HALF + HALF // 2

conf_rate = 0.5
ridge_weight = 0.5

bf16 = jnp.bfloat16
f32 = jnp.float32


def dot(a, b):
    return lax.dot_general(a, b, (((1,), (0,)), ((), ())), preferred_element_type=f32)


def split(a):
    hi = a.astype(bf16)
    return hi, (a - hi.astype(f32)).astype(bf16)


def offsets(live_ref, base):
    out = [0]
    for p in range(PAIRS - 1):
        out.append(out[-1] + live_ref[base + p])
    return out


COUNT_AT = PAIRS
ITEM_AT = COUNT_AT + PAIRS
BLOCK_AT = ITEM_AT + GROUPS * PAIRS
LIVE_AT = BLOCK_AT + GROUPS
PACK = LIVE_AT + GROUPS


def fetch(pairs, sems):
    copies = [pltpu.make_async_copy(src, dst, sems.at[i]) for i, (src, dst) in enumerate(pairs)]
    for copy in copies:
        copy.start()
    for copy in copies:
        copy.wait()


def square(rows):
    return lax.dot_general(rows, rows, (((0,), (0,)), ((), ())), preferred_element_type=f32)


def pack_kernel(slots_ref, blocks_ref, out_ref):
    out_ref[...] = jnp.zeros(out_ref.shape, f32)
    items = slots_ref[:, 2 * PAIRS :, :].reshape(GROUPS * PAIRS, NNZ)
    for d in range(C * X):
        out_ref[d, : 2 * PAIRS, :NNZ] = slots_ref[d % X, : 2 * PAIRS, :]
        out_ref[d, ITEM_AT : ITEM_AT + GROUPS * PAIRS, :NNZ] = items
        out_ref[d, BLOCK_AT:, :PAIRS] = blocks_ref[...]


def unpack_kernel(core_ref, part_ref, pack_ref, after_ref, own_ref, live_ref):
    for c in range(C):
        own_ref[c] = pack_ref[c * X + part_ref[0], BLOCK_AT:PACK, :].astype(jnp.int32)
    for s in range(X):
        row = pack_ref[core_ref[0] * X + s, pl.ds(LIVE_AT + part_ref[0], 1), :]
        live_ref[s : s + 1, :] = row.astype(jnp.int32)


def weight_kernel(core_ref, live_ref, pack_ref, out_ref, rows_ref):
    packs = [pack_ref[core_ref[0] * X + s] for s in range(X)]
    users = [pack[:PAIRS] for pack in packs]
    counts = [pack[COUNT_AT : COUNT_AT + PAIRS] for pack in packs]
    table = jnp.concatenate(users + counts, axis=0).T[:NNZ]
    lane = lax.broadcasted_iota(jnp.int32, (NNZ, BLK), 1).astype(f32)
    slot = lax.broadcasted_iota(jnp.int32, (NNZ, BLK), 0)
    for s in range(X):
        offs = offsets(live_ref, s * PAIRS)
        for p in range(PAIRS):
            q = s * PAIRS + p
            hit = (table[:, q : q + 1] == lane) & (slot < live_ref[q])
            rows = jnp.where(hit, table[:, X * PAIRS + q : X * PAIRS + q + 1], 0.0)
            rows_ref[s, pl.ds(offs[p], NNZ), :] = rows
        out_ref[s * LIVE : (s + 1) * LIVE, :] = rows_ref[s, :LIVE, :].astype(bf16)


def place_kernel(part_ref, seen_ref, live_ref, pack_ref, out_ref, rows_ref):
    items = [
        pack_ref[c * X + part_ref[0], ITEM_AT : ITEM_AT + GROUPS * PAIRS, :] for c in range(C)
    ]
    table = jnp.concatenate(items, axis=0).T[:NNZ].astype(jnp.int32)
    lane = lax.broadcasted_iota(jnp.int32, (LIVE, BLK), 1)
    slot = lax.broadcasted_iota(jnp.int32, (NNZ, 1), 0)
    merged = jnp.full((LIVE, BLK), -1, jnp.int32)
    for d in range(C * GROUPS):
        offs = offsets(live_ref, d * PAIRS)
        for p in range(PAIRS):
            q = d * PAIRS + p
            spot = jnp.where(slot < seen_ref[q], table[:, q : q + 1] + p * BLK, -1)
            rows_ref[d, pl.ds(offs[p], NNZ), :] = jnp.broadcast_to(spot, (NNZ, BLK))
        merged = jnp.where(lane == d, rows_ref[d, :LIVE, :], merged)
    out_ref[...] = merged


def collect_kernel(turn_ref, block_ref, *refs):
    piece_refs, (out_ref, gram_ref, held, sems) = refs[:-4], refs[-4:]
    fetch([(piece_ref, held.at[i]) for i, piece_ref in enumerate(piece_refs)], sems)
    for q in range(C * GROUPS * PAIRS):
        turn = turn_ref[q]
        place = jnp.minimum(jnp.where(turn > Y // 2, turn - 1, turn), Y - 2)
        out_ref[q] = held[place, block_ref[q]]
    gram = square(held[0].reshape(Z * BLK, E))
    for i in range(1, Y - 1):
        gram = gram + square(held[i].reshape(Z * BLK, E))
    gram_ref[...] = gram


def select_kernel(
    turn_ref, block_ref, place_ref, gram_ref, held_ref, last_hbm, out_ref, last_ref, sems
):
    fetch([(last_hbm, last_ref)], sems)
    gram = gram_ref[...] + square(last_ref[...].reshape(Z * BLK, E))
    corner = gram[:HALF, HALF:]
    gram = jnp.concatenate(
        [
            jnp.concatenate([gram[:HALF, :HALF], gram[HALF:, HALF:]], axis=1),
            jnp.concatenate([corner[: HALF // 2], corner[HALF // 2 :]], axis=1),
        ],
        axis=0,
    )
    gram_hi, gram_lo = split(gram)
    lane = lax.broadcasted_iota(jnp.int32, (LIVE, PAIRS * BLK), 1)
    for d in range(C * GROUPS):
        blocks = []
        for p in range(PAIRS):
            q = d * PAIRS + p
            blocks.append(
                jnp.where(turn_ref[q] == Y // 2, last_ref[block_ref[q]], held_ref[q])
            )
        onehot = jnp.where(place_ref[:, d : d + 1] == lane, 1.0, 0.0).astype(bf16)
        rows = dot(onehot, jnp.concatenate(blocks, axis=0))
        out_ref[d, :LIVE, :] = rows.astype(bf16)
        out_ref[d, LIVE : LIVE + GRAM, :] = gram_hi
        out_ref[d, LIVE + GRAM :, :] = gram_lo


def merge_kernel(halves_ref, out_ref):
    gram = jnp.zeros((GRAM, E), f32)
    for c in range(C):
        for part in range(2):
            at = LIVE + part * GRAM
            gram = gram + halves_ref[c, 0, at : at + GRAM, :].astype(f32)
    gram_hi, gram_lo = split(gram)
    for g in range(GROUPS):
        out_ref[g, :LIVE, :] = halves_ref[0, g, :LIVE, :] + halves_ref[1, g, :LIVE, :]
        out_ref[g, LIVE : LIVE + GRAM, :] = gram_hi
        out_ref[g, LIVE + GRAM :, :] = gram_lo


def solve_kernel(recv_ref, weight_ref, start_ref, out_ref):
    items = recv_ref[:, :LIVE, :].reshape(X * LIVE, E)
    items_t = items.T
    weight = weight_ref[...]
    conf = weight.astype(f32) * conf_rate
    full = jnp.where(weight > 0, 1.0 + conf, 0.0).astype(bf16)
    gram = recv_ref[:, LIVE : LIVE + GRAM, :].astype(f32) + recv_ref[:, LIVE + GRAM :, :].astype(f32)
    gram = jnp.sum(gram, axis=0)
    corner = jnp.concatenate([gram[HALF:, :HALF], gram[HALF:, HALF:]], axis=0)
    gram = jnp.concatenate(
        [
            jnp.concatenate([gram[:HALF, :HALF], corner], axis=1),
            jnp.concatenate([corner.T, gram[:HALF, HALF:]], axis=1),
        ],
        axis=0,
    )
    eye = lax.broadcasted_iota(jnp.int32, (E, E), 0) == lax.broadcasted_iota(jnp.int32, (E, E), 1)
    base_hi, base_lo = split(
        gram * (E / (X * Z * Y * C * BLK)) + jnp.where(eye, ridge_weight, 0.0)
    )

    def operator(vectors):
        hi, lo = split(vectors)
        both = jnp.concatenate([hi, lo], axis=1)
        table = dot(items, both)
        table = conf * (table[:, :BLK] + table[:, BLK:])
        table_hi, table_lo = split(table)
        summed = dot(items_t, jnp.concatenate([table_hi, table_lo], axis=1))
        dense = dot(base_hi, both)
        return (
            (summed[:, :BLK] + summed[:, BLK:])
            + (dense[:, :BLK] + dense[:, BLK:])
            + dot(base_lo, hi)
        )

    x = start_ref[...].T
    remain = dot(items_t, full) - operator(x)
    direction = remain
    norm_now = jnp.sum(remain * remain, axis=0, keepdims=True)
    for turn in range(ITERS):
        image = operator(direction)
        step = norm_now / jnp.sum(direction * image, axis=0, keepdims=True)
        x = x + step * direction
        if turn < ITERS - 1:
            remain = remain - step * image
            norm_next = jnp.sum(remain * remain, axis=0, keepdims=True)
            direction = remain + norm_next / norm_now * direction
            norm_now = norm_next
    out_ref[...] = x.T.astype(out_ref.dtype)


def vmem():
    return pl.BlockSpec(memory_space=pltpu.VMEM)


def smem():
    return pl.BlockSpec(memory_space=pltpu.SMEM)


def hbm():
    return pl.BlockSpec(memory_space=pl.ANY)


def spread(value, axis, size):
    return lax.all_to_all(jnp.broadcast_to(value[None], (size,) + value.shape), axis, 0, 0, tiled=True)


def from_next(value):
    return lax.ppermute(value, "y", [(i, (i - 1) % Y) for i in range(Y)])


def from_last(value):
    return lax.ppermute(value, "y", [(i, (i + 1) % Y) for i in range(Y)])


def call(kernel, out, ins, scratch=(), flops=1_000_000, nbytes=400_000):
    return pl.pallas_call(
        kernel,
        out_shape=out,
        in_specs=ins,
        out_specs=[vmem() for _ in out] if isinstance(out, tuple) else vmem(),
        scratch_shapes=list(scratch),
        compiler_params=pltpu.CompilerParams(vmem_limit_bytes=24 * 1024 * 1024),
        cost_estimate=pl.CostEstimate(flops=flops, bytes_accessed=nbytes, transcendentals=0),
    )


def local(block_ids, pair_live, user_rows, item_rows, counts, item_emb, user_emb):
    core = lax.axis_index("core")
    part = lax.axis_index("x")
    own_block = item_emb[0].astype(bf16)
    with jax.named_scope("gather_z"):
        column = lax.all_gather(own_block, "z", axis=0, tiled=True)
    with jax.named_scope("gather_y"):
        ups, downs = [column], [column]
        for _ in range(Y // 2 - 1):
            ups.append(from_next(ups[-1]))
            downs.append(from_last(downs[-1]))
        downs.append(from_last(downs[-1]))
        pieces = [piece.reshape(Z, BLK, E) for piece in ups + downs[:0:-1]]

    with jax.named_scope("small_exchange"):
        slots = jnp.concatenate([user_rows[:, 0], counts[:, 0], item_rows[:, 0]], axis=1)
        blocks = jnp.concatenate([block_ids[:, 0], pair_live[:, 0]], axis=0)
        pack = call(
            pack_kernel, jax.ShapeDtypeStruct((C * X, PACK, BLK), f32), [vmem()] * 2
        )(slots.astype(f32), blocks.astype(f32))
        pack = lax.all_to_all(pack, ("core", "x"), 0, 0, tiled=True)
        own, user_live = call(
            unpack_kernel,
            (
                jax.ShapeDtypeStruct((C, PACK - BLOCK_AT, BLK), jnp.int32),
                jax.ShapeDtypeStruct((X, BLK), jnp.int32),
            ),
            [smem()] * 2 + [vmem(), hbm()],
        )(core.reshape(1), part.reshape(1), pack, downs[-2])

    with jax.named_scope("indices"):
        own, user_live = own[:, :, :PAIRS], user_live[:, :PAIRS].reshape(-1)
        ids, live = own[:, :GROUPS].reshape(-1), own[:, GROUPS:].reshape(-1)
        z_of, y_of, c_of = ids // (Y * C), ids // C % Y, ids % C
        turns = (y_of - lax.axis_index("y")) % Y
        spots = jnp.clip(z_of, 0, Z - 1)
        seen = jnp.where(c_of == core, live, 0)

    with jax.named_scope("place"):
        place = call(
            place_kernel,
            jax.ShapeDtypeStruct((LIVE, BLK), jnp.int32),
            [smem()] * 3 + [vmem()],
            [pltpu.VMEM((C * GROUPS, LIVE + NNZ, BLK), jnp.int32)],
        )(part.reshape(1), seen, live, pack)
    with jax.named_scope("weights"):
        weight = call(
            weight_kernel,
            jax.ShapeDtypeStruct((X * LIVE, BLK), bf16),
            [smem()] * 2 + [vmem()],
            [pltpu.VMEM((X, LIVE + NNZ, BLK), f32)],
        )(core.reshape(1), user_live, pack)
    with jax.named_scope("collect"):
        last = pieces.pop(Y // 2)
        held, gram = call(
            collect_kernel,
            (
                jax.ShapeDtypeStruct((C * GROUPS * PAIRS, BLK, E), bf16),
                jax.ShapeDtypeStruct((E, E), f32),
            ),
            [smem()] * 2 + [hbm()] * len(pieces),
            [
                pltpu.VMEM((Y - 1, Z, BLK, E), bf16),
                pltpu.SemaphoreType.DMA((Y - 1,)),
            ],
            nbytes=4_000_000,
        )(turns, spots, *pieces)
    with jax.named_scope("select"):
        chosen = call(
            select_kernel,
            jax.ShapeDtypeStruct((C * GROUPS, LIVE + 2 * GRAM, E), bf16),
            [smem()] * 2 + [vmem()] * 3 + [hbm()],
            [pltpu.VMEM((Z, BLK, E), bf16), pltpu.SemaphoreType.DMA((1,))],
            flops=700_000_000,
            nbytes=4_000_000,
        )(turns, spots, place, gram, held, last)
    with jax.named_scope("exchange"):
        halves = lax.all_to_all(
            chosen.reshape((C, GROUPS) + chosen.shape[1:]), "core", 0, 0, tiled=True
        )
        merged = call(merge_kernel, jax.ShapeDtypeStruct(halves.shape[1:], bf16), [vmem()])(halves)
        received = lax.all_to_all(merged, "x", 0, 0, tiled=True)
    with jax.named_scope("solve"):
        start = lax.dynamic_slice_in_dim(user_emb, part * BLK, BLK, 0)
        solved = call(
            solve_kernel,
            jax.ShapeDtypeStruct((BLK, E), bf16),
            [vmem()] * 3,
            flops=800_000_000,
            nbytes=1_200_000,
        )(received, weight, start)
    with jax.named_scope("gather_x"):
        return spread(solved, "x", X).reshape(X * BLK, E).astype(f32)


def solution(mesh):
    grid = Mesh(mesh.devices.reshape(Z, Y, C, X), ("z", "y", "core", "x"))
    users = ("z", "y", "core")
    return jax.shard_map(
        local,
        mesh=grid,
        in_specs=(
            P(users, "x", None),
            P(users, "x", None),
            P(users, "x", None, None),
            P(users, "x", None, None),
            P(users, "x", None, None),
            P("x", users, None),
            P(users, None),
        ),
        out_specs=P(users, None),
        check_vma=False,
    )
```

```python
import functools

import jax
import jax.numpy as jnp
from jax import lax
from jax.experimental import pallas as pl
from jax.experimental.pallas import tpu as pltpu
from jax.sharding import Mesh, PartitionSpec as P

Z, Y, C, X = 12, 8, 2, 4
E = 128
BLK = 128
PAIRS = 8
NNZ = 64
LIVE = 320
ITERS = 3
GROUPS = 4
HALF = E // 2
GRAM = HALF + HALF // 2

conf_rate = 0.5
ridge_weight = 0.5

bf16 = jnp.bfloat16
f32 = jnp.float32


def dot(a, b):
    return lax.dot_general(a, b, (((1,), (0,)), ((), ())), preferred_element_type=f32)


def split(a):
    hi = a.astype(bf16)
    return hi, (a - hi.astype(f32)).astype(bf16)


def offsets(live_ref, base):
    out = [0]
    for p in range(PAIRS - 1):
        out.append(out[-1] + live_ref[base + p])
    return out


COUNT_AT = PAIRS
ITEM_AT = COUNT_AT + PAIRS
BLOCK_AT = ITEM_AT + GROUPS * PAIRS
LIVE_AT = BLOCK_AT + GROUPS
PACK = LIVE_AT + GROUPS


def fetch(pairs, sems):
    copies = [pltpu.make_async_copy(src, dst, sems.at[i]) for i, (src, dst) in enumerate(pairs)]
    for copy in copies:
        copy.start()
    for copy in copies:
        copy.wait()


def square(rows):
    return lax.dot_general(rows, rows, (((0,), (0,)), ((), ())), preferred_element_type=f32)


def pack_kernel(slots_ref, blocks_ref, out_ref):
    out_ref[...] = jnp.zeros(out_ref.shape, f32)
    items = slots_ref[:, 2 * PAIRS :, :].reshape(GROUPS * PAIRS, NNZ)
    for d in range(C * X):
        out_ref[d, : 2 * PAIRS, :NNZ] = slots_ref[d % X, : 2 * PAIRS, :]
        out_ref[d, ITEM_AT : ITEM_AT + GROUPS * PAIRS, :NNZ] = items
        out_ref[d, BLOCK_AT:, :PAIRS] = blocks_ref[...]


def unpack_kernel(core_ref, part_ref, pack_ref, after_ref, own_ref, live_ref):
    for c in range(C):
        source = (core_ref[0] + c) % C * X + part_ref[0]
        own_ref[c] = pack_ref[source, BLOCK_AT:PACK, :].astype(jnp.int32)
    for s in range(X):
        row = pack_ref[core_ref[0] * X + s, pl.ds(LIVE_AT + part_ref[0], 1), :]
        live_ref[s : s + 1, :] = row.astype(jnp.int32)


def weight_kernel(core_ref, live_ref, pack_ref, out_ref, rows_ref):
    packs = [pack_ref[core_ref[0] * X + s] for s in range(X)]
    users = [pack[:PAIRS] for pack in packs]
    counts = [pack[COUNT_AT : COUNT_AT + PAIRS] for pack in packs]
    table = jnp.concatenate(users + counts, axis=0).T[:NNZ]
    lane = lax.broadcasted_iota(jnp.int32, (NNZ, BLK), 1).astype(f32)
    slot = lax.broadcasted_iota(jnp.int32, (NNZ, BLK), 0)
    for s in range(X):
        offs = offsets(live_ref, s * PAIRS)
        for p in range(PAIRS):
            q = s * PAIRS + p
            hit = (table[:, q : q + 1] == lane) & (slot < live_ref[q])
            rows = jnp.where(hit, table[:, X * PAIRS + q : X * PAIRS + q + 1], 0.0)
            rows_ref[s, pl.ds(offs[p], NNZ), :] = rows
        out_ref[s * LIVE : (s + 1) * LIVE, :] = rows_ref[s, :LIVE, :].astype(bf16)


def place_kernel(core_ref, part_ref, seen_ref, live_ref, pack_ref, out_ref, rows_ref):
    items = [
        pack_ref[
            (core_ref[0] + c) % C * X + part_ref[0], ITEM_AT : ITEM_AT + GROUPS * PAIRS, :
        ]
        for c in range(C)
    ]
    table = jnp.concatenate(items, axis=0).T[:NNZ].astype(jnp.int32)
    lane = lax.broadcasted_iota(jnp.int32, (LIVE, BLK), 1)
    slot = lax.broadcasted_iota(jnp.int32, (NNZ, 1), 0)
    merged = jnp.full((LIVE, BLK), -1, jnp.int32)
    for d in range(C * GROUPS):
        offs = offsets(live_ref, d * PAIRS)
        for p in range(PAIRS):
            q = d * PAIRS + p
            spot = jnp.where(slot < seen_ref[q], table[:, q : q + 1] + p * BLK, -1)
            rows_ref[d, pl.ds(offs[p], NNZ), :] = jnp.broadcast_to(spot, (NNZ, BLK))
        merged = jnp.where(lane == d, rows_ref[d, :LIVE, :], merged)
    out_ref[...] = merged


def collect_kernel(turn_ref, block_ref, *refs):
    piece_refs, (out_ref, gram_ref, held, sems) = refs[:-4], refs[-4:]
    fetch([(piece_ref, held.at[i]) for i, piece_ref in enumerate(piece_refs)], sems)
    for q in range(C * GROUPS * PAIRS):
        turn = turn_ref[q]
        place = jnp.minimum(jnp.where(turn > Y // 2, turn - 1, turn), Y - 2)
        out_ref[q] = held[place, block_ref[q]]
    gram = square(held[0].reshape(Z * BLK, E))
    for i in range(1, Y - 1):
        gram = gram + square(held[i].reshape(Z * BLK, E))
    gram_ref[...] = gram


def select_rows(first, turn_ref, block_ref, place_ref, held_ref, last_ref, out_ref):
    lane = lax.broadcasted_iota(jnp.int32, (LIVE, PAIRS * BLK), 1)
    for g in range(GROUPS):
        blocks = []
        for p in range(PAIRS):
            q = (first + g) * PAIRS + p
            blocks.append(
                jnp.where(turn_ref[q] == Y // 2, last_ref[block_ref[q]], held_ref[q])
            )
        onehot = jnp.where(place_ref[:, first + g : first + g + 1] == lane, 1.0, 0.0).astype(bf16)
        rows = dot(onehot, jnp.concatenate(blocks, axis=0))
        out_ref[g, :LIVE, :] = rows.astype(bf16)


def select_other_kernel(
    turn_ref, block_ref, place_ref, gram_ref, held_ref, last_hbm, out_ref, packed_ref, last_ref, sems
):
    fetch([(last_hbm, last_ref)], sems)
    select_rows(GROUPS, turn_ref, block_ref, place_ref, held_ref, last_ref, out_ref)
    gram = gram_ref[...] + square(last_ref[...].reshape(Z * BLK, E))
    corner = gram[:HALF, HALF:]
    gram = jnp.concatenate(
        [
            jnp.concatenate([gram[:HALF, :HALF], gram[HALF:, HALF:]], axis=1),
            jnp.concatenate([corner[: HALF // 2], corner[HALF // 2 :]], axis=1),
        ],
        axis=0,
    )
    packed_ref[...] = gram
    gram_hi, gram_lo = split(gram)
    for g in range(GROUPS):
        out_ref[g, LIVE : LIVE + GRAM, :] = gram_hi
        out_ref[g, LIVE + GRAM :, :] = gram_lo


def select_own_kernel(turn_ref, block_ref, place_ref, held_ref, last_hbm, out_ref, last_ref, sems):
    fetch([(last_hbm, last_ref)], sems)
    select_rows(0, turn_ref, block_ref, place_ref, held_ref, last_ref, out_ref)


def merge_kernel(own_ref, packed_ref, other_ref, out_ref):
    gram = other_ref[0, LIVE : LIVE + GRAM, :].astype(f32) + other_ref[0, LIVE + GRAM :, :].astype(f32)
    gram_hi, gram_lo = split(packed_ref[...] + gram)
    for g in range(GROUPS):
        out_ref[g, :LIVE, :] = own_ref[g] + other_ref[g, :LIVE, :]
        out_ref[g, LIVE : LIVE + GRAM, :] = gram_hi
        out_ref[g, LIVE + GRAM :, :] = gram_lo


def solve_kernel(recv_ref, weight_ref, start_ref, out_ref):
    items = recv_ref[:, :LIVE, :].reshape(X * LIVE, E)
    items_t = items.T
    weight = weight_ref[...]
    conf = weight.astype(f32) * conf_rate
    full = jnp.where(weight > 0, 1.0 + conf, 0.0).astype(bf16)
    gram = recv_ref[:, LIVE : LIVE + GRAM, :].astype(f32) + recv_ref[:, LIVE + GRAM :, :].astype(f32)
    gram = jnp.sum(gram, axis=0)
    corner = jnp.concatenate([gram[HALF:, :HALF], gram[HALF:, HALF:]], axis=0)
    gram = jnp.concatenate(
        [
            jnp.concatenate([gram[:HALF, :HALF], corner], axis=1),
            jnp.concatenate([corner.T, gram[:HALF, HALF:]], axis=1),
        ],
        axis=0,
    )
    eye = lax.broadcasted_iota(jnp.int32, (E, E), 0) == lax.broadcasted_iota(jnp.int32, (E, E), 1)
    base_hi, base_lo = split(
        gram * (E / (X * Z * Y * C * BLK)) + jnp.where(eye, ridge_weight, 0.0)
    )

    def operator(vectors):
        hi, lo = split(vectors)
        both = jnp.concatenate([hi, lo], axis=1)
        table = dot(items, both)
        table = conf * (table[:, :BLK] + table[:, BLK:])
        table_hi, table_lo = split(table)
        summed = dot(items_t, jnp.concatenate([table_hi, table_lo], axis=1))
        dense = dot(base_hi, both)
        return (
            (summed[:, :BLK] + summed[:, BLK:])
            + (dense[:, :BLK] + dense[:, BLK:])
            + dot(base_lo, hi)
        )

    x = start_ref[...].T
    remain = dot(items_t, full) - operator(x)
    direction = remain
    norm_now = jnp.sum(remain * remain, axis=0, keepdims=True)
    for turn in range(ITERS):
        image = operator(direction)
        step = norm_now / jnp.sum(direction * image, axis=0, keepdims=True)
        x = x + step * direction
        if turn < ITERS - 1:
            remain = remain - step * image
            norm_next = jnp.sum(remain * remain, axis=0, keepdims=True)
            direction = remain + norm_next / norm_now * direction
            norm_now = norm_next
    out_ref[...] = x.T.astype(out_ref.dtype)


def vmem():
    return pl.BlockSpec(memory_space=pltpu.VMEM)


def smem():
    return pl.BlockSpec(memory_space=pltpu.SMEM)


def hbm():
    return pl.BlockSpec(memory_space=pl.ANY)


def spread(value, axis, size):
    return lax.all_to_all(jnp.broadcast_to(value[None], (size,) + value.shape), axis, 0, 0, tiled=True)


def from_next(value):
    return lax.ppermute(value, "y", [(i, (i - 1) % Y) for i in range(Y)])


def from_last(value):
    return lax.ppermute(value, "y", [(i, (i + 1) % Y) for i in range(Y)])


def call(kernel, out, ins, scratch=(), flops=1_000_000, nbytes=400_000):
    return pl.pallas_call(
        kernel,
        out_shape=out,
        in_specs=ins,
        out_specs=[vmem() for _ in out] if isinstance(out, tuple) else vmem(),
        scratch_shapes=list(scratch),
        compiler_params=pltpu.CompilerParams(vmem_limit_bytes=24 * 1024 * 1024),
        cost_estimate=pl.CostEstimate(flops=flops, bytes_accessed=nbytes, transcendentals=0),
    )


def local(block_ids, pair_live, user_rows, item_rows, counts, item_emb, user_emb):
    core = lax.axis_index("core")
    part = lax.axis_index("x")
    own_block = item_emb[0].astype(bf16)
    with jax.named_scope("gather_z"):
        column = lax.all_gather(own_block, "z", axis=0, tiled=True)
    with jax.named_scope("gather_y"):
        ups, downs = [column], [column]
        for _ in range(Y // 2 - 1):
            ups.append(from_next(ups[-1]))
            downs.append(from_last(downs[-1]))
        downs.append(from_last(downs[-1]))
        pieces = [piece.reshape(Z, BLK, E) for piece in ups + downs[:0:-1]]

    with jax.named_scope("small_exchange"):
        slots = jnp.concatenate([user_rows[:, 0], counts[:, 0], item_rows[:, 0]], axis=1)
        blocks = jnp.concatenate([block_ids[:, 0], pair_live[:, 0]], axis=0)
        pack = call(
            pack_kernel, jax.ShapeDtypeStruct((C * X, PACK, BLK), f32), [vmem()] * 2
        )(slots.astype(f32), blocks.astype(f32))
        pack = lax.all_to_all(pack, ("core", "x"), 0, 0, tiled=True)
        own, user_live = call(
            unpack_kernel,
            (
                jax.ShapeDtypeStruct((C, PACK - BLOCK_AT, BLK), jnp.int32),
                jax.ShapeDtypeStruct((X, BLK), jnp.int32),
            ),
            [smem()] * 2 + [vmem(), hbm()],
        )(core.reshape(1), part.reshape(1), pack, downs[-2])

    with jax.named_scope("indices"):
        own, user_live = own[:, :, :PAIRS], user_live[:, :PAIRS].reshape(-1)
        ids, live = own[:, :GROUPS].reshape(-1), own[:, GROUPS:].reshape(-1)
        z_of, y_of, c_of = ids // (Y * C), ids // C % Y, ids % C
        turns = (y_of - lax.axis_index("y")) % Y
        spots = jnp.clip(z_of, 0, Z - 1)
        seen = jnp.where(c_of == core, live, 0)

    with jax.named_scope("place"):
        place = call(
            place_kernel,
            jax.ShapeDtypeStruct((LIVE, BLK), jnp.int32),
            [smem()] * 4 + [vmem()],
            [pltpu.VMEM((C * GROUPS, LIVE + NNZ, BLK), jnp.int32)],
        )(core.reshape(1), part.reshape(1), seen, live, pack)
    with jax.named_scope("weights"):
        weight = call(
            weight_kernel,
            jax.ShapeDtypeStruct((X * LIVE, BLK), bf16),
            [smem()] * 2 + [vmem()],
            [pltpu.VMEM((X, LIVE + NNZ, BLK), f32)],
        )(core.reshape(1), user_live, pack)
    with jax.named_scope("collect"):
        last = pieces.pop(Y // 2)
        held, gram = call(
            collect_kernel,
            (
                jax.ShapeDtypeStruct((C * GROUPS * PAIRS, BLK, E), bf16),
                jax.ShapeDtypeStruct((E, E), f32),
            ),
            [smem()] * 2 + [hbm()] * len(pieces),
            [
                pltpu.VMEM((Y - 1, Z, BLK, E), bf16),
                pltpu.SemaphoreType.DMA((Y - 1,)),
            ],
            nbytes=4_000_000,
        )(turns, spots, *pieces)
    with jax.named_scope("select"):
        shape = jax.ShapeDtypeStruct((GROUPS, LIVE + 2 * GRAM, E), bf16)
        scratch = [pltpu.VMEM((Z, BLK, E), bf16), pltpu.SemaphoreType.DMA((1,))]
        other, packed = call(
            select_other_kernel,
            (shape, jax.ShapeDtypeStruct((GRAM, E), f32)),
            [smem()] * 2 + [vmem()] * 3 + [hbm()],
            scratch,
            flops=350_000_000,
            nbytes=2_000_000,
        )(turns, spots, place, gram, held, last)
        other = lax.ppermute(other, "core", [(c, (c + 1) % C) for c in range(C)])
        chosen = call(
            select_own_kernel,
            jax.ShapeDtypeStruct((GROUPS, LIVE, E), bf16),
            [smem()] * 2 + [vmem()] * 2 + [hbm()],
            scratch,
            flops=350_000_000,
            nbytes=2_000_000,
        )(turns, spots, place, held, last)
    with jax.named_scope("exchange"):
        merged = call(merge_kernel, shape, [vmem()] * 3)(chosen, packed, other)
        received = lax.all_to_all(merged, "x", 0, 0, tiled=True)
    with jax.named_scope("solve"):
        start = lax.dynamic_slice_in_dim(user_emb, part * BLK, BLK, 0)
        solved = call(
            solve_kernel,
            jax.ShapeDtypeStruct((BLK, E), bf16),
            [vmem()] * 3,
            flops=800_000_000,
            nbytes=1_200_000,
        )(received, weight, start)
    with jax.named_scope("gather_x"):
        return spread(solved, "x", X).reshape(X * BLK, E).astype(f32)


def solution(mesh):
    grid = Mesh(mesh.devices.reshape(Z, Y, C, X), ("z", "y", "core", "x"))
    users = ("z", "y", "core")
    return jax.shard_map(
        local,
        mesh=grid,
        in_specs=(
            P(users, "x", None),
            P(users, "x", None),
            P(users, "x", None, None),
            P(users, "x", None, None),
            P(users, "x", None, None),
            P("x", users, None),
            P(users, None),
        ),
        out_specs=P(users, None),
        check_vma=False,
    )
```

```python
import functools

import jax
import jax.numpy as jnp
from jax import lax
from jax.experimental import pallas as pl
from jax.experimental.pallas import tpu as pltpu
from jax.sharding import Mesh, PartitionSpec as P

Z, Y, C, X = 12, 8, 2, 4
E = 128
BLK = 128
PAIRS = 8
NNZ = 64
LIVE = 320
ITERS = 3
GROUPS = 4
HALF = E // 2
GRAM = HALF + HALF // 2

conf_rate = 0.5
ridge_weight = 0.5

bf16 = jnp.bfloat16
f32 = jnp.float32


def dot(a, b):
    return lax.dot_general(a, b, (((1,), (0,)), ((), ())), preferred_element_type=f32)


def split(a):
    hi = a.astype(bf16)
    return hi, (a - hi.astype(f32)).astype(bf16)


def offsets(live_ref, base):
    out = [0]
    for p in range(PAIRS - 1):
        out.append(out[-1] + live_ref[base + p])
    return out


COUNT_AT = PAIRS
ITEM_AT = COUNT_AT + PAIRS
BLOCK_AT = ITEM_AT + GROUPS * PAIRS
LIVE_AT = BLOCK_AT + GROUPS
PACK = LIVE_AT + GROUPS


def fetch(pairs, sems):
    copies = [pltpu.make_async_copy(src, dst, sems.at[i]) for i, (src, dst) in enumerate(pairs)]
    for copy in copies:
        copy.start()
    for copy in copies:
        copy.wait()


def square(rows):
    return lax.dot_general(rows, rows, (((0,), (0,)), ((), ())), preferred_element_type=f32)


def pack_kernel(slots_ref, blocks_ref, out_ref):
    out_ref[...] = jnp.zeros(out_ref.shape, f32)
    items = slots_ref[:, 2 * PAIRS :, :].reshape(GROUPS * PAIRS, NNZ)
    for d in range(C * X):
        out_ref[d, : 2 * PAIRS, :NNZ] = slots_ref[d % X, : 2 * PAIRS, :]
        out_ref[d, ITEM_AT : ITEM_AT + GROUPS * PAIRS, :NNZ] = items
        out_ref[d, BLOCK_AT:, :PAIRS] = blocks_ref[...]


def unpack_kernel(core_ref, part_ref, pack_ref, after_ref, own_ref, live_ref):
    for c in range(C):
        source = (core_ref[0] + c) % C * X + part_ref[0]
        own_ref[c] = pack_ref[source, BLOCK_AT:PACK, :].astype(jnp.int32)
    for s in range(X):
        row = pack_ref[core_ref[0] * X + s, pl.ds(LIVE_AT + part_ref[0], 1), :]
        live_ref[s : s + 1, :] = row.astype(jnp.int32)


def weight_kernel(core_ref, live_ref, pack_ref, out_ref, rows_ref):
    packs = [pack_ref[core_ref[0] * X + s] for s in range(X)]
    users = [pack[:PAIRS] for pack in packs]
    counts = [pack[COUNT_AT : COUNT_AT + PAIRS] for pack in packs]
    table = jnp.concatenate(users + counts, axis=0).T[:NNZ]
    lane = lax.broadcasted_iota(jnp.int32, (NNZ, BLK), 1).astype(f32)
    slot = lax.broadcasted_iota(jnp.int32, (NNZ, BLK), 0)
    for s in range(X):
        offs = offsets(live_ref, s * PAIRS)
        for p in range(PAIRS):
            q = s * PAIRS + p
            hit = (table[:, q : q + 1] == lane) & (slot < live_ref[q])
            rows = jnp.where(hit, table[:, X * PAIRS + q : X * PAIRS + q + 1], 0.0)
            rows_ref[s, pl.ds(offs[p], NNZ), :] = rows
        out_ref[s * LIVE : (s + 1) * LIVE, :] = rows_ref[s, :LIVE, :].astype(bf16)


def place_kernel(core_ref, part_ref, seen_ref, live_ref, pack_ref, out_ref, rows_ref):
    items = [
        pack_ref[
            (core_ref[0] + c) % C * X + part_ref[0], ITEM_AT : ITEM_AT + GROUPS * PAIRS, :
        ]
        for c in range(C)
    ]
    table = jnp.concatenate(items, axis=0).T[:NNZ].astype(jnp.int32)
    lane = lax.broadcasted_iota(jnp.int32, (LIVE, BLK), 1)
    slot = lax.broadcasted_iota(jnp.int32, (NNZ, 1), 0)
    merged = jnp.full((LIVE, BLK), -1, jnp.int32)
    for d in range(C * GROUPS):
        offs = offsets(live_ref, d * PAIRS)
        for p in range(PAIRS):
            q = d * PAIRS + p
            spot = jnp.where(slot < seen_ref[q], table[:, q : q + 1] + p * BLK, -1)
            rows_ref[d, pl.ds(offs[p], NNZ), :] = jnp.broadcast_to(spot, (NNZ, BLK))
        merged = jnp.where(lane == d, rows_ref[d, :LIVE, :], merged)
    out_ref[...] = merged


def collect_kernel(turn_ref, block_ref, *refs):
    piece_refs, (out_ref, gram_ref, held, sems) = refs[:-4], refs[-4:]
    fetch([(piece_ref, held.at[i]) for i, piece_ref in enumerate(piece_refs)], sems)
    for q in range(C * GROUPS * PAIRS):
        turn = turn_ref[q]
        place = jnp.minimum(jnp.where(turn > Y // 2, turn - 1, turn), Y - 2)
        out_ref[q] = held[place, block_ref[q]]
    gram = square(held[0].reshape(Z * BLK, E))
    for i in range(1, Y - 1):
        gram = gram + square(held[i].reshape(Z * BLK, E))
    gram_ref[...] = gram


def select_rows(first, turn_ref, block_ref, place_ref, held_ref, last_ref, out_ref):
    lane = lax.broadcasted_iota(jnp.int32, (LIVE, PAIRS * BLK), 1)
    for g in range(GROUPS):
        blocks = []
        for p in range(PAIRS):
            q = (first + g) * PAIRS + p
            blocks.append(
                jnp.where(turn_ref[q] == Y // 2, last_ref[block_ref[q]], held_ref[q])
            )
        onehot = jnp.where(place_ref[:, first + g : first + g + 1] == lane, 1.0, 0.0).astype(bf16)
        rows = dot(onehot, jnp.concatenate(blocks, axis=0))
        out_ref[g, :LIVE, :] = rows.astype(bf16)


def select_other_kernel(
    turn_ref, block_ref, place_ref, gram_ref, held_ref, last_hbm, out_ref, packed_ref, last_ref, sems
):
    fetch([(last_hbm, last_ref)], sems)
    select_rows(GROUPS, turn_ref, block_ref, place_ref, held_ref, last_ref, out_ref)
    gram = gram_ref[...] + square(last_ref[...].reshape(Z * BLK, E))
    corner = gram[:HALF, HALF:]
    gram = jnp.concatenate(
        [
            jnp.concatenate([gram[:HALF, :HALF], gram[HALF:, HALF:]], axis=1),
            jnp.concatenate([corner[: HALF // 2], corner[HALF // 2 :]], axis=1),
        ],
        axis=0,
    )
    packed_ref[...] = gram
    gram_hi, gram_lo = split(gram)
    for g in range(GROUPS):
        out_ref[g, LIVE : LIVE + GRAM, :] = gram_hi
        out_ref[g, LIVE + GRAM :, :] = gram_lo


def select_own_kernel(turn_ref, block_ref, place_ref, held_ref, last_hbm, out_ref, last_ref, sems):
    fetch([(last_hbm, last_ref)], sems)
    select_rows(0, turn_ref, block_ref, place_ref, held_ref, last_ref, out_ref)


def merge_kernel(own_ref, packed_ref, other_ref, out_ref):
    gram = other_ref[0, LIVE : LIVE + GRAM, :].astype(f32) + other_ref[0, LIVE + GRAM :, :].astype(f32)
    gram_hi, gram_lo = split(packed_ref[...] + gram)
    for g in range(GROUPS):
        out_ref[g, :LIVE, :] = own_ref[g] + other_ref[g, :LIVE, :]
        out_ref[g, LIVE : LIVE + GRAM, :] = gram_hi
        out_ref[g, LIVE + GRAM :, :] = gram_lo


def solve_kernel(recv_ref, weight_ref, start_ref, out_ref):
    items = recv_ref[:, :LIVE, :].reshape(X * LIVE, E)
    items_t = items.T
    weight = weight_ref[...]
    conf = weight.astype(f32) * conf_rate
    full = jnp.where(weight > 0, 1.0 + conf, 0.0).astype(bf16)
    gram = recv_ref[:, LIVE : LIVE + GRAM, :].astype(f32) + recv_ref[:, LIVE + GRAM :, :].astype(f32)
    gram = jnp.sum(gram, axis=0)
    corner = jnp.concatenate([gram[HALF:, :HALF], gram[HALF:, HALF:]], axis=0)
    gram = jnp.concatenate(
        [
            jnp.concatenate([gram[:HALF, :HALF], corner], axis=1),
            jnp.concatenate([corner.T, gram[:HALF, HALF:]], axis=1),
        ],
        axis=0,
    )
    eye = lax.broadcasted_iota(jnp.int32, (E, E), 0) == lax.broadcasted_iota(jnp.int32, (E, E), 1)
    base_hi, base_lo = split(
        gram * (E / (X * Z * Y * C * BLK)) + jnp.where(eye, ridge_weight, 0.0)
    )

    def operator(vectors):
        hi, lo = split(vectors)
        both = jnp.concatenate([hi, lo], axis=1)
        table = dot(items, both)
        table = conf * (table[:, :BLK] + table[:, BLK:])
        table_hi, table_lo = split(table)
        summed = dot(items_t, jnp.concatenate([table_hi, table_lo], axis=1))
        dense = dot(base_hi, both)
        return (
            (summed[:, :BLK] + summed[:, BLK:])
            + (dense[:, :BLK] + dense[:, BLK:])
            + dot(base_lo, hi)
        )

    x = start_ref[...].T
    remain = dot(items_t, full) - operator(x)
    direction = remain
    norm_now = jnp.sum(remain * remain, axis=0, keepdims=True)
    for turn in range(ITERS):
        image = operator(direction)
        step = norm_now / jnp.sum(direction * image, axis=0, keepdims=True)
        x = x + step * direction
        if turn < ITERS - 1:
            remain = remain - step * image
            norm_next = jnp.sum(remain * remain, axis=0, keepdims=True)
            direction = remain + norm_next / norm_now * direction
            norm_now = norm_next
    out_ref[...] = x.T.astype(out_ref.dtype)


def vmem():
    return pl.BlockSpec(memory_space=pltpu.VMEM)


def smem():
    return pl.BlockSpec(memory_space=pltpu.SMEM)


def hbm():
    return pl.BlockSpec(memory_space=pl.ANY)


def spread(value, axis, size):
    return lax.all_to_all(jnp.broadcast_to(value[None], (size,) + value.shape), axis, 0, 0, tiled=True)


def from_next(value):
    return lax.ppermute(value, "y", [(i, (i - 1) % Y) for i in range(Y)])


def from_last(value):
    return lax.ppermute(value, "y", [(i, (i + 1) % Y) for i in range(Y)])


def call(kernel, out, ins, scratch=(), flops=1_000_000, nbytes=400_000):
    return pl.pallas_call(
        kernel,
        out_shape=out,
        in_specs=ins,
        out_specs=[vmem() for _ in out] if isinstance(out, tuple) else vmem(),
        scratch_shapes=list(scratch),
        compiler_params=pltpu.CompilerParams(vmem_limit_bytes=24 * 1024 * 1024),
        cost_estimate=pl.CostEstimate(flops=flops, bytes_accessed=nbytes, transcendentals=0),
    )


def pass_kernel(value_ref, after_ref, out_ref):
    pass


def pass_on(value, after):
    return pl.pallas_call(
        pass_kernel,
        out_shape=jax.ShapeDtypeStruct(value.shape, value.dtype),
        in_specs=[hbm(), hbm()],
        out_specs=hbm(),
        input_output_aliases={0: 0},
    )(value, after)


def local(block_ids, pair_live, user_rows, item_rows, counts, item_emb, user_emb):
    core = lax.axis_index("core")
    part = lax.axis_index("x")
    own_block = item_emb[0].astype(bf16)
    with jax.named_scope("gather_z"):
        column = lax.all_gather(own_block, "z", axis=0, tiled=True)
    with jax.named_scope("small_exchange"):
        slots = jnp.concatenate([user_rows[:, 0], counts[:, 0], item_rows[:, 0]], axis=1)
        blocks = jnp.concatenate([block_ids[:, 0], pair_live[:, 0]], axis=0)
        pack = call(
            pack_kernel, jax.ShapeDtypeStruct((C * X, PACK, BLK), f32), [vmem()] * 2
        )(slots.astype(f32), blocks.astype(f32))
    with jax.named_scope("gather_y"):
        ups, downs = [column], [column]
        for _ in range(Y // 2 - 1):
            ups.append(from_next(ups[-1]))
            downs.append(from_last(downs[-1]))
            if len(ups) == 2:
                ups[1] = pass_on(ups[1], pack)
        downs.append(from_last(downs[-1]))
        pieces = [piece.reshape(Z, BLK, E) for piece in ups + downs[:0:-1]]

    with jax.named_scope("small_exchange"):
        pack = lax.all_to_all(pack, ("core", "x"), 0, 0, tiled=True)
        own, user_live = call(
            unpack_kernel,
            (
                jax.ShapeDtypeStruct((C, PACK - BLOCK_AT, BLK), jnp.int32),
                jax.ShapeDtypeStruct((X, BLK), jnp.int32),
            ),
            [smem()] * 2 + [vmem(), hbm()],
        )(core.reshape(1), part.reshape(1), pack, downs[-2])

    with jax.named_scope("indices"):
        own, user_live = own[:, :, :PAIRS], user_live[:, :PAIRS].reshape(-1)
        ids, live = own[:, :GROUPS].reshape(-1), own[:, GROUPS:].reshape(-1)
        z_of, y_of, c_of = ids // (Y * C), ids // C % Y, ids % C
        turns = (y_of - lax.axis_index("y")) % Y
        spots = jnp.clip(z_of, 0, Z - 1)
        seen = jnp.where(c_of == core, live, 0)

    with jax.named_scope("place"):
        place = call(
            place_kernel,
            jax.ShapeDtypeStruct((LIVE, BLK), jnp.int32),
            [smem()] * 4 + [vmem()],
            [pltpu.VMEM((C * GROUPS, LIVE + NNZ, BLK), jnp.int32)],
        )(core.reshape(1), part.reshape(1), seen, live, pack)
    with jax.named_scope("weights"):
        weight = call(
            weight_kernel,
            jax.ShapeDtypeStruct((X * LIVE, BLK), bf16),
            [smem()] * 2 + [vmem()],
            [pltpu.VMEM((X, LIVE + NNZ, BLK), f32)],
        )(core.reshape(1), user_live, pack)
    with jax.named_scope("collect"):
        last = pieces.pop(Y // 2)
        held, gram = call(
            collect_kernel,
            (
                jax.ShapeDtypeStruct((C * GROUPS * PAIRS, BLK, E), bf16),
                jax.ShapeDtypeStruct((E, E), f32),
            ),
            [smem()] * 2 + [hbm()] * len(pieces),
            [
                pltpu.VMEM((Y - 1, Z, BLK, E), bf16),
                pltpu.SemaphoreType.DMA((Y - 1,)),
            ],
            nbytes=4_000_000,
        )(turns, spots, *pieces)
    with jax.named_scope("select"):
        shape = jax.ShapeDtypeStruct((GROUPS, LIVE + 2 * GRAM, E), bf16)
        scratch = [pltpu.VMEM((Z, BLK, E), bf16), pltpu.SemaphoreType.DMA((1,))]
        other, packed = call(
            select_other_kernel,
            (shape, jax.ShapeDtypeStruct((GRAM, E), f32)),
            [smem()] * 2 + [vmem()] * 3 + [hbm()],
            scratch,
            flops=350_000_000,
            nbytes=2_000_000,
        )(turns, spots, place, gram, held, last)
        other = lax.ppermute(other, "core", [(c, (c + 1) % C) for c in range(C)])
        chosen = call(
            select_own_kernel,
            jax.ShapeDtypeStruct((GROUPS, LIVE, E), bf16),
            [smem()] * 2 + [vmem()] * 2 + [hbm()],
            scratch,
            flops=350_000_000,
            nbytes=2_000_000,
        )(turns, spots, place, held, last)
    with jax.named_scope("exchange"):
        merged = call(merge_kernel, shape, [vmem()] * 3)(chosen, packed, other)
        received = lax.all_to_all(merged, "x", 0, 0, tiled=True)
    with jax.named_scope("solve"):
        start = lax.dynamic_slice_in_dim(user_emb, part * BLK, BLK, 0)
        solved = call(
            solve_kernel,
            jax.ShapeDtypeStruct((BLK, E), bf16),
            [vmem()] * 3,
            flops=800_000_000,
            nbytes=1_200_000,
        )(received, weight, start)
    with jax.named_scope("gather_x"):
        return spread(solved, "x", X).reshape(X * BLK, E).astype(f32)


def solution(mesh):
    grid = Mesh(mesh.devices.reshape(Z, Y, C, X), ("z", "y", "core", "x"))
    users = ("z", "y", "core")
    return jax.shard_map(
        local,
        mesh=grid,
        in_specs=(
            P(users, "x", None),
            P(users, "x", None),
            P(users, "x", None, None),
            P(users, "x", None, None),
            P(users, "x", None, None),
            P("x", users, None),
            P(users, None),
        ),
        out_specs=P(users, None),
        check_vma=False,
    )
```

```python
import functools

import jax
import jax.numpy as jnp
from jax import lax
from jax.experimental import pallas as pl
from jax.experimental.pallas import tpu as pltpu
from jax.sharding import Mesh, PartitionSpec as P

Z, Y, C, X = 12, 8, 2, 4
E = 128
BLK = 128
PAIRS = 8
NNZ = 64
LIVE = 320
ITERS = 3
GROUPS = 4
HALF = E // 2
GRAM = HALF + HALF // 2

conf_rate = 0.5
ridge_weight = 0.5

bf16 = jnp.bfloat16
f32 = jnp.float32


def dot(a, b):
    return lax.dot_general(a, b, (((1,), (0,)), ((), ())), preferred_element_type=f32)


def split(a):
    hi = a.astype(bf16)
    return hi, (a - hi.astype(f32)).astype(bf16)


def offsets(live_ref, base):
    out = [0]
    for p in range(PAIRS - 1):
        out.append(out[-1] + live_ref[base + p])
    return out


COUNT_AT = PAIRS
ITEM_AT = COUNT_AT + PAIRS
BLOCK_AT = ITEM_AT + GROUPS * PAIRS
LIVE_AT = BLOCK_AT + GROUPS
PACK = LIVE_AT + GROUPS


def fetch(pairs, sems):
    copies = [pltpu.make_async_copy(src, dst, sems.at[i]) for i, (src, dst) in enumerate(pairs)]
    for copy in copies:
        copy.start()
    for copy in copies:
        copy.wait()


def square(rows):
    return lax.dot_general(rows, rows, (((0,), (0,)), ((), ())), preferred_element_type=f32)


def pack_kernel(slots_ref, blocks_ref, out_ref):
    out_ref[...] = jnp.zeros(out_ref.shape, f32)
    items = slots_ref[:, 2 * PAIRS :, :].reshape(GROUPS * PAIRS, NNZ)
    for d in range(C * X):
        out_ref[d, : 2 * PAIRS, :NNZ] = slots_ref[d % X, : 2 * PAIRS, :]
        out_ref[d, ITEM_AT : ITEM_AT + GROUPS * PAIRS, :NNZ] = items
        out_ref[d, BLOCK_AT:, :PAIRS] = blocks_ref[...]


def unpack_kernel(core_ref, part_ref, pack_ref, after_ref, own_ref, live_ref):
    for c in range(C):
        source = (core_ref[0] + c) % C * X + part_ref[0]
        own_ref[c] = pack_ref[source, BLOCK_AT:PACK, :].astype(jnp.int32)
    for s in range(X):
        row = pack_ref[core_ref[0] * X + s, pl.ds(LIVE_AT + part_ref[0], 1), :]
        live_ref[s : s + 1, :] = row.astype(jnp.int32)


def weight_kernel(core_ref, live_ref, pack_ref, out_ref, rows_ref):
    packs = [pack_ref[core_ref[0] * X + s] for s in range(X)]
    users = [pack[:PAIRS] for pack in packs]
    counts = [pack[COUNT_AT : COUNT_AT + PAIRS] for pack in packs]
    table = jnp.concatenate(users + counts, axis=0).T[:NNZ]
    lane = lax.broadcasted_iota(jnp.int32, (NNZ, BLK), 1).astype(f32)
    slot = lax.broadcasted_iota(jnp.int32, (NNZ, BLK), 0)
    for s in range(X):
        offs = offsets(live_ref, s * PAIRS)
        for p in range(PAIRS):
            q = s * PAIRS + p
            hit = (table[:, q : q + 1] == lane) & (slot < live_ref[q])
            rows = jnp.where(hit, table[:, X * PAIRS + q : X * PAIRS + q + 1], 0.0)
            rows_ref[s, pl.ds(offs[p], NNZ), :] = rows
        out_ref[s * LIVE : (s + 1) * LIVE, :] = rows_ref[s, :LIVE, :].astype(bf16)


def place_kernel(core_ref, part_ref, seen_ref, live_ref, pack_ref, out_ref, rows_ref):
    items = [
        pack_ref[
            (core_ref[0] + c) % C * X + part_ref[0], ITEM_AT : ITEM_AT + GROUPS * PAIRS, :
        ]
        for c in range(C)
    ]
    table = jnp.concatenate(items, axis=0).T[:NNZ].astype(jnp.int32)
    lane = lax.broadcasted_iota(jnp.int32, (LIVE, BLK), 1)
    slot = lax.broadcasted_iota(jnp.int32, (NNZ, 1), 0)
    merged = jnp.full((LIVE, BLK), -1, jnp.int32)
    for d in range(C * GROUPS):
        offs = offsets(live_ref, d * PAIRS)
        for p in range(PAIRS):
            q = d * PAIRS + p
            spot = jnp.where(slot < seen_ref[q], table[:, q : q + 1] + p * BLK, -1)
            rows_ref[d, pl.ds(offs[p], NNZ), :] = jnp.broadcast_to(spot, (NNZ, BLK))
        merged = jnp.where(lane == d, rows_ref[d, :LIVE, :], merged)
    out_ref[...] = merged


def collect_kernel(turn_ref, block_ref, after_ref, *refs):
    piece_refs, (out_ref, gram_ref, held, sems) = refs[:-4], refs[-4:]
    fetch([(piece_ref, held.at[i]) for i, piece_ref in enumerate(piece_refs)], sems)
    for q in range(C * GROUPS * PAIRS):
        turn = turn_ref[q]
        place = jnp.minimum(jnp.where(turn > Y // 2, turn - 1, turn), Y - 2)
        out_ref[q] = held[place, block_ref[q]]
    gram = square(held[0].reshape(Z * BLK, E))
    for i in range(1, Y - 1):
        gram = gram + square(held[i].reshape(Z * BLK, E))
    gram_ref[...] = gram


def select_rows(first, turn_ref, block_ref, place_ref, held_ref, last_ref, out_ref):
    lane = lax.broadcasted_iota(jnp.int32, (LIVE, PAIRS * BLK), 1)
    for g in range(GROUPS):
        blocks = []
        for p in range(PAIRS):
            q = (first + g) * PAIRS + p
            blocks.append(
                jnp.where(turn_ref[q] == Y // 2, last_ref[block_ref[q]], held_ref[q])
            )
        onehot = jnp.where(place_ref[:, first + g : first + g + 1] == lane, 1.0, 0.0).astype(bf16)
        rows = dot(onehot, jnp.concatenate(blocks, axis=0))
        out_ref[g, :LIVE, :] = rows.astype(bf16)


def select_other_kernel(
    turn_ref, block_ref, place_ref, gram_ref, held_ref, last_hbm, out_ref, packed_ref, last_ref, sems
):
    fetch([(last_hbm, last_ref)], sems)
    select_rows(GROUPS, turn_ref, block_ref, place_ref, held_ref, last_ref, out_ref)
    gram = gram_ref[...] + square(last_ref[...].reshape(Z * BLK, E))
    corner = gram[:HALF, HALF:]
    gram = jnp.concatenate(
        [
            jnp.concatenate([gram[:HALF, :HALF], gram[HALF:, HALF:]], axis=1),
            jnp.concatenate([corner[: HALF // 2], corner[HALF // 2 :]], axis=1),
        ],
        axis=0,
    )
    packed_ref[...] = gram
    gram_hi, gram_lo = split(gram)
    for g in range(GROUPS):
        out_ref[g, LIVE : LIVE + GRAM, :] = gram_hi
        out_ref[g, LIVE + GRAM :, :] = gram_lo


def select_own_kernel(turn_ref, block_ref, place_ref, held_ref, last_hbm, out_ref, last_ref, sems):
    fetch([(last_hbm, last_ref)], sems)
    select_rows(0, turn_ref, block_ref, place_ref, held_ref, last_ref, out_ref)


def merge_kernel(own_ref, packed_ref, other_ref, out_ref):
    gram = other_ref[0, LIVE : LIVE + GRAM, :].astype(f32) + other_ref[0, LIVE + GRAM :, :].astype(f32)
    gram_hi, gram_lo = split(packed_ref[...] + gram)
    for g in range(GROUPS):
        out_ref[g, :LIVE, :] = own_ref[g] + other_ref[g, :LIVE, :]
        out_ref[g, LIVE : LIVE + GRAM, :] = gram_hi
        out_ref[g, LIVE + GRAM :, :] = gram_lo


def solve_kernel(recv_ref, weight_ref, start_ref, out_ref):
    items = recv_ref[:, :LIVE, :].reshape(X * LIVE, E)
    items_t = items.T
    weight = weight_ref[...]
    conf = weight.astype(f32) * conf_rate
    full = jnp.where(weight > 0, 1.0 + conf, 0.0).astype(bf16)
    gram = recv_ref[:, LIVE : LIVE + GRAM, :].astype(f32) + recv_ref[:, LIVE + GRAM :, :].astype(f32)
    gram = jnp.sum(gram, axis=0)
    corner = jnp.concatenate([gram[HALF:, :HALF], gram[HALF:, HALF:]], axis=0)
    gram = jnp.concatenate(
        [
            jnp.concatenate([gram[:HALF, :HALF], corner], axis=1),
            jnp.concatenate([corner.T, gram[:HALF, HALF:]], axis=1),
        ],
        axis=0,
    )
    eye = lax.broadcasted_iota(jnp.int32, (E, E), 0) == lax.broadcasted_iota(jnp.int32, (E, E), 1)
    base_hi, base_lo = split(
        gram * (E / (X * Z * Y * C * BLK)) + jnp.where(eye, ridge_weight, 0.0)
    )

    def operator(vectors):
        hi, lo = split(vectors)
        both = jnp.concatenate([hi, lo], axis=1)
        table = dot(items, both)
        table = conf * (table[:, :BLK] + table[:, BLK:])
        table_hi, table_lo = split(table)
        summed = dot(items_t, jnp.concatenate([table_hi, table_lo], axis=1))
        dense = dot(base_hi, both)
        return (
            (summed[:, :BLK] + summed[:, BLK:])
            + (dense[:, :BLK] + dense[:, BLK:])
            + dot(base_lo, hi)
        )

    x = start_ref[...].T
    remain = dot(items_t, full) - operator(x)
    direction = remain
    norm_now = jnp.sum(remain * remain, axis=0, keepdims=True)
    for turn in range(ITERS):
        image = operator(direction)
        step = norm_now / jnp.sum(direction * image, axis=0, keepdims=True)
        x = x + step * direction
        if turn < ITERS - 1:
            remain = remain - step * image
            norm_next = jnp.sum(remain * remain, axis=0, keepdims=True)
            direction = remain + norm_next / norm_now * direction
            norm_now = norm_next
    out_ref[...] = x.T.astype(out_ref.dtype)


def vmem():
    return pl.BlockSpec(memory_space=pltpu.VMEM)


def smem():
    return pl.BlockSpec(memory_space=pltpu.SMEM)


def hbm():
    return pl.BlockSpec(memory_space=pl.ANY)


def spread(value, axis, size):
    return lax.all_to_all(jnp.broadcast_to(value[None], (size,) + value.shape), axis, 0, 0, tiled=True)


def from_next(value):
    return lax.ppermute(value, "y", [(i, (i - 1) % Y) for i in range(Y)])


def from_last(value):
    return lax.ppermute(value, "y", [(i, (i + 1) % Y) for i in range(Y)])


def call(kernel, out, ins, scratch=(), flops=1_000_000, nbytes=400_000):
    return pl.pallas_call(
        kernel,
        out_shape=out,
        in_specs=ins,
        out_specs=[vmem() for _ in out] if isinstance(out, tuple) else vmem(),
        scratch_shapes=list(scratch),
        compiler_params=pltpu.CompilerParams(vmem_limit_bytes=24 * 1024 * 1024),
        cost_estimate=pl.CostEstimate(flops=flops, bytes_accessed=nbytes, transcendentals=0),
    )


def pass_kernel(value_ref, after_ref, out_ref):
    pass


def pass_on(value, after):
    return pl.pallas_call(
        pass_kernel,
        out_shape=jax.ShapeDtypeStruct(value.shape, value.dtype),
        in_specs=[hbm(), hbm()],
        out_specs=hbm(),
        input_output_aliases={0: 0},
    )(value, after)


def local(block_ids, pair_live, user_rows, item_rows, counts, item_emb, user_emb):
    core = lax.axis_index("core")
    part = lax.axis_index("x")
    own_block = item_emb[0].astype(bf16)
    with jax.named_scope("gather_z"):
        column = lax.all_gather(own_block, "z", axis=0, tiled=True)
    with jax.named_scope("small_exchange"):
        slots = jnp.concatenate([user_rows[:, 0], counts[:, 0], item_rows[:, 0]], axis=1)
        blocks = jnp.concatenate([block_ids[:, 0], pair_live[:, 0]], axis=0)
        pack = call(
            pack_kernel, jax.ShapeDtypeStruct((C * X, PACK, BLK), f32), [vmem()] * 2
        )(slots.astype(f32), blocks.astype(f32))
    with jax.named_scope("gather_y"):
        ups, downs = [column], [column]
        for _ in range(Y // 2 - 1):
            ups.append(from_next(ups[-1]))
            downs.append(from_last(downs[-1]))
            if len(ups) == 2:
                ups[1] = pass_on(ups[1], pack)
        downs.append(from_last(downs[-1]))
        pieces = [piece.reshape(Z, BLK, E) for piece in ups + downs[:0:-1]]

    with jax.named_scope("small_exchange"):
        pack = lax.all_to_all(pack, ("core", "x"), 0, 0, tiled=True)
        own, user_live = call(
            unpack_kernel,
            (
                jax.ShapeDtypeStruct((C, PACK - BLOCK_AT, BLK), jnp.int32),
                jax.ShapeDtypeStruct((X, BLK), jnp.int32),
            ),
            [smem()] * 2 + [vmem(), hbm()],
        )(core.reshape(1), part.reshape(1), pack, downs[-2])

    with jax.named_scope("indices"):
        own, user_live = own[:, :, :PAIRS], user_live[:, :PAIRS].reshape(-1)
        ids, live = own[:, :GROUPS].reshape(-1), own[:, GROUPS:].reshape(-1)
        z_of, y_of, c_of = ids // (Y * C), ids // C % Y, ids % C
        turns = (y_of - lax.axis_index("y")) % Y
        spots = jnp.clip(z_of, 0, Z - 1)
        seen = jnp.where(c_of == core, live, 0)

    with jax.named_scope("place"):
        place = call(
            place_kernel,
            jax.ShapeDtypeStruct((LIVE, BLK), jnp.int32),
            [smem()] * 4 + [vmem()],
            [pltpu.VMEM((C * GROUPS, LIVE + NNZ, BLK), jnp.int32)],
        )(core.reshape(1), part.reshape(1), seen, live, pack)
    with jax.named_scope("weights"):
        weight = call(
            weight_kernel,
            jax.ShapeDtypeStruct((X * LIVE, BLK), bf16),
            [smem()] * 2 + [vmem()],
            [pltpu.VMEM((X, LIVE + NNZ, BLK), f32)],
        )(core.reshape(1), user_live, pack)
    with jax.named_scope("collect"):
        last = pieces.pop(Y // 2)
        held, gram = call(
            collect_kernel,
            (
                jax.ShapeDtypeStruct((C * GROUPS * PAIRS, BLK, E), bf16),
                jax.ShapeDtypeStruct((E, E), f32),
            ),
            [smem()] * 2 + [hbm()] * (1 + len(pieces)),
            [
                pltpu.VMEM((Y - 1, Z, BLK, E), bf16),
                pltpu.SemaphoreType.DMA((Y - 1,)),
            ],
            nbytes=4_000_000,
        )(turns, spots, place, *pieces)
    with jax.named_scope("select"):
        shape = jax.ShapeDtypeStruct((GROUPS, LIVE + 2 * GRAM, E), bf16)
        scratch = [pltpu.VMEM((Z, BLK, E), bf16), pltpu.SemaphoreType.DMA((1,))]
        other, packed = call(
            select_other_kernel,
            (shape, jax.ShapeDtypeStruct((GRAM, E), f32)),
            [smem()] * 2 + [vmem()] * 3 + [hbm()],
            scratch,
            flops=350_000_000,
            nbytes=2_000_000,
        )(turns, spots, place, gram, held, last)
        other = lax.ppermute(other, "core", [(c, (c + 1) % C) for c in range(C)])
        chosen = call(
            select_own_kernel,
            jax.ShapeDtypeStruct((GROUPS, LIVE, E), bf16),
            [smem()] * 2 + [vmem()] * 2 + [hbm()],
            scratch,
            flops=350_000_000,
            nbytes=2_000_000,
        )(turns, spots, place, held, last)
    with jax.named_scope("exchange"):
        merged = call(merge_kernel, shape, [vmem()] * 3)(chosen, packed, other)
        received = lax.all_to_all(merged, "x", 0, 0, tiled=True)
    with jax.named_scope("solve"):
        start = lax.dynamic_slice_in_dim(user_emb, part * BLK, BLK, 0)
        solved = call(
            solve_kernel,
            jax.ShapeDtypeStruct((BLK, E), bf16),
            [vmem()] * 3,
            flops=800_000_000,
            nbytes=1_200_000,
        )(received, weight, start)
    with jax.named_scope("gather_x"):
        return spread(solved, "x", X).reshape(X * BLK, E).astype(f32)


def solution(mesh):
    grid = Mesh(mesh.devices.reshape(Z, Y, C, X), ("z", "y", "core", "x"))
    users = ("z", "y", "core")
    return jax.shard_map(
        local,
        mesh=grid,
        in_specs=(
            P(users, "x", None),
            P(users, "x", None),
            P(users, "x", None, None),
            P(users, "x", None, None),
            P(users, "x", None, None),
            P("x", users, None),
            P(users, None),
        ),
        out_specs=P(users, None),
        check_vma=False,
    )
```
